32 devices in a mesh: dp: 4 (over x, core), mp: 4 (over z), rep: 2 (over y).
Axes of the slice: x: 2, y: 2, z: 4, core: 2. Of those that a mesh axis runs over, the one named last changes fastest.
Arguments:
- query_rows: bfloat16 [512, 1280], P(('dp', 'mp', 'rep')), may hold values from -64 to 64
- key_rows: bfloat16 [512, 1280], P(('dp', 'mp', 'rep')), may hold values from -7 to 7
- value_rows: bfloat16 [512, 1280], P(('dp', 'mp', 'rep')), may hold values from -6 to 6
- residual: bfloat16 [512, 1280], P(('dp', 'mp', 'rep')), may hold values from -6 to 6
- out_proj: bfloat16 [1280, 1280], replicated, may hold values from -0.15625 to 0.15625
- merge_gain: float32 [1280], replicated, may hold values from 0.1 to 1.9
- merger_proj: bfloat16 [5120, 8192], P(None, ('mp', 'rep')), may hold values from -1.5 to 1.5
- model_gain: float32 [8192], P(('mp', 'rep')), may hold values from 0.1 to 1.9
- image_grid: int32 [32, 2], replicated, may hold values from 1 to 4, as said below
- image_group: int32 [32], replicated, may hold values from 0 to 3, as said below
- rollout_image: int32 [512], P('dp'), may hold values from 0 to 31, as said below
- cotangent: bfloat16 [2048, 8192], P('dp', ('mp', 'rep')), may hold values from -0.078125 to 0.078125
Outputs:
- normed_tokens: bfloat16 [128, 8192], P('dp', ('mp', 'rep'))
- merger_grad: float32 [5120, 8192], P('dp', ('mp', 'rep'))
The draws below stay inside these ranges and needn't reach their ends.
Inputs may be any that keep to these rules, and one draw needn't show every extreme that they name: `image_grid`: height times width of every image is between 1 and 4; image 0 has height 4 and width 1. `image_group`: every rollout group receives exactly 8 images. Among the 8 images of one owner group (images k * 8 to k * 8 + 7) at most 3 go to any one rollout group, and every owner group sends exactly 3 to some rollout group. `rollout_image`: rollouts come in blocks of 128, one block a rollout group in order of group; every image has exactly 16 rollouts, all in the block of its image_group.
All inputs are finite; a program needn't handle non-finite values.
Results may differ from the reference program's by a relative error of at most 0.02.
Values may be sent and summed in bfloat16 or wider, within the bound.
No kernel may reach another device: no remote copies, remote signals or barrier semaphores. Data moves between devices by JAX's collectives and lax.ppermute only.
A program may use at most 64 MiB of HBM per device.

```python
import jax
import jax.numpy as jnp
import numpy as np
from jax import lax

DV = 1280
HEADS = 16
D = 8192
IMG_TOK = 4
ROLL = 16
HEAD = 80
DM = 5120
PATCH_SLOTS = 16
IMAGES = 32
GROUPS = 4
IMGS_G = 8
CAP = 3
ROLLOUTS = 512
PATCHES = 512


def routing_plan(key):
    per_shift = np.clip(IMGS_G - np.arange(GROUPS) * CAP, 0, CAP)
    shift_list = np.repeat(np.arange(GROUPS), per_shift).astype(np.int32)
    shifts = jax.random.permutation(jax.random.fold_in(key, 71), jnp.asarray(shift_list, dtype=jnp.int32))
    labels = jax.random.permutation(jax.random.fold_in(key, 72), GROUPS).astype(jnp.int32)
    owners = jnp.arange(GROUPS, dtype=jnp.int32)[:, None]
    destination = labels[(owners + shifts[None, :]) % GROUPS].reshape(-1).astype(jnp.int32)
    image_order = jnp.argsort(destination, stable=True).astype(jnp.int32).reshape(GROUPS, IMGS_G)
    repeated = jnp.repeat(image_order, ROLL, axis=1)
    width_all = IMGS_G * ROLL
    scores = jax.random.randint(jax.random.fold_in(key, 73), (GROUPS, width_all), 0, 65536, dtype=jnp.int32)
    scores = scores * width_all + jnp.arange(width_all, dtype=jnp.int32)[None, :]
    shuffle = jnp.argsort(scores, axis=1)
    rollouts = jnp.take_along_axis(repeated, shuffle, axis=1).reshape(-1).astype(jnp.int32)
    return (destination, rollouts)


def draw_image_group(key, part):
    return routing_plan(key)[0]


def draw_rollout_image(key, part):
    return routing_plan(key)[1]


def draw_image_grid(key, part):
    wide_seed, tall_seed = jax.random.split(jax.random.fold_in(key, 81))
    grid_wide = jnp.minimum(jax.random.randint(wide_seed, (IMAGES,), 1, 3, dtype=jnp.int32), IMG_TOK)
    highest = IMG_TOK // grid_wide
    grid_tall = 1 + jax.random.randint(tall_seed, (IMAGES,), 0, 1 << 20, dtype=jnp.int32) % highest
    grid_wide = grid_wide.at[0].set(1)
    grid_tall = grid_tall.at[0].set(IMG_TOK)
    return jnp.stack([grid_tall, grid_wide], axis=1).astype(jnp.int32)


def attention_pair(key):
    query_seed, key_seed = jax.random.split(jax.random.fold_in(key, 91))
    queries = jax.random.truncated_normal(query_seed, -6.0, 6.0, (PATCHES, DV), jnp.float32)
    keys_all = jax.random.truncated_normal(key_seed, -6.0, 6.0, (PATCHES, DV), jnp.float32)
    return (queries, keys_all)


def draw_query_rows(key, part):
    return attention_pair(key)[0].astype(jnp.bfloat16)


def draw_key_rows(key, part):
    return attention_pair(key)[1].astype(jnp.bfloat16)


def draw_merger_proj(key, part):
    weight_seed, column_seed = jax.random.split(jax.random.fold_in(key, 101))
    column = jnp.arange(D, dtype=jnp.float32) / D
    jitter = jax.random.truncated_normal(column_seed, -2.0, 2.0, (D,), jnp.float32)
    ramp = 10.0 ** column * jnp.exp(0.25 * jitter) / 4.64
    values_all = jax.random.truncated_normal(weight_seed, -6.0, 6.0, (DM, D), jnp.float32)
    return (values_all * ramp[None, :] * DM ** (-0.5)).astype(jnp.bfloat16)


def steps_of(own_key, extent, pieces, smallest, largest):
    level, own = 1.0, jax.random.fold_in(own_key, 6)
    for dim, shards_of in pieces:
        draws = jnp.exp(jax.random.uniform(jax.random.fold_in(own, dim), (shards_of,), jnp.float32, smallest / len(pieces), largest / len(pieces)))
        level = level * jnp.repeat(draws, extent[dim] // shards_of).reshape([-1 if axis == dim else 1 for axis in range(len(extent))])
    return level


def bell_draw(key, dims, width, limit, cuts=(), kind=jnp.bfloat16):
    factor_of = steps_of(key, dims, cuts, -0.22, 0.18) if cuts else 1.0
    result = jax.random.normal(key, dims, jnp.float32) * width * factor_of
    return jnp.minimum(jnp.maximum(result, -limit), limit).astype(kind)


def setup_inputs(seed: int = 0) -> dict:
    key_of = jax.random.split(jax.random.key(seed), 13)
    query_rows = draw_query_rows(jax.random.fold_in(key_of[12], 71), 0)
    key_rows = draw_key_rows(jax.random.fold_in(key_of[12], 71), 0)
    value_rows = bell_draw(key_of[2], (PATCHES, DV), 1.0, 6.0, ((0, 32),))
    residual = bell_draw(key_of[3], (PATCHES, DV), 1.0, 6.0, ((0, 32),))
    out_proj = bell_draw(key_of[4], (DV, DV), DV ** -0.5, 0.15625)
    merge_gain = jnp.clip(1.0 + 0.18 * jax.random.normal(key_of[5], (DV,), jnp.float32), 0.1, 1.9)
    merger_proj = draw_merger_proj(jax.random.fold_in(key_of[12], 71), 0)
    model_gain = jnp.clip(1.0 + 0.18 * jax.random.normal(key_of[7], (D,), jnp.float32), 0.1, 1.9)
    image_grid = draw_image_grid(jax.random.fold_in(key_of[12], 71), 0)
    image_group = draw_image_group(jax.random.fold_in(key_of[12], 71), 0)
    rollout_image = draw_rollout_image(jax.random.fold_in(key_of[12], 71), 0)
    cotangent = bell_draw(key_of[11], (ROLLOUTS * IMG_TOK, D), 0.005, 0.078125, ((0, 4), (1, 8)))
    return dict(query_rows=query_rows, key_rows=key_rows, value_rows=value_rows, residual=residual, out_proj=out_proj, merge_gain=merge_gain, merger_proj=merger_proj, model_gain=model_gain, image_grid=image_grid, image_group=image_group, rollout_image=rollout_image, cotangent=cotangent)


EPSILON = 1e-06

def reference(query_rows, key_rows, value_rows, residual, out_proj, merge_gain, merger_proj, model_gain, image_grid, image_group, rollout_image, cotangent):
    counts = (image_grid[:, 0] * image_grid[:, 1]).astype(jnp.int32)
    patch_valid = jnp.arange(PATCH_SLOTS, dtype=jnp.int32)[None, :] < 4 * counts[:, None]
    query_heads = query_rows.astype(jnp.float32).reshape(IMAGES, PATCH_SLOTS, HEADS, HEAD)
    key_heads = key_rows.astype(jnp.float32).reshape(IMAGES, PATCH_SLOTS, HEADS, HEAD)
    value_heads = value_rows.astype(jnp.float32).reshape(IMAGES, PATCH_SLOTS, HEADS, HEAD)
    scores = jnp.einsum('iphd,ikhd->ihpk', query_heads, key_heads) * HEAD ** (-0.5)
    scores = jnp.where(patch_valid[:, None, None, :], scores, -1e+30)
    attn_weights = jax.nn.softmax(scores, axis=-1).astype(jnp.bfloat16)
    attended = jnp.einsum('ihpk,ikhd->iphd', attn_weights.astype(jnp.float32), value_heads)
    attended = attended.astype(jnp.bfloat16).reshape(IMAGES * PATCH_SLOTS, DV)
    mixed_rows = residual.astype(jnp.float32) + jnp.dot(attended, out_proj, preferred_element_type=jnp.float32)
    inverse_rms = lax.rsqrt(lax.optimization_barrier(jnp.mean(mixed_rows * mixed_rows, axis=-1, keepdims=True)) + EPSILON)
    valid_rows = patch_valid.reshape(-1, 1).astype(jnp.float32)
    merged = (mixed_rows * inverse_rms * merge_gain * valid_rows).astype(jnp.bfloat16).reshape(IMAGES * IMG_TOK, DM)
    projected = jnp.dot(merged, merger_proj, preferred_element_type=jnp.float32).astype(jnp.bfloat16)
    image_order = jnp.argsort(image_group, stable=True).astype(jnp.int32)
    model_input = projected.reshape(IMAGES, IMG_TOK, D)[image_order]
    hidden = model_input.astype(jnp.float32)
    inverse = lax.rsqrt(lax.optimization_barrier(jnp.sum(hidden * hidden, axis=-1)) / D + EPSILON)
    normed_tokens = (hidden * inverse[..., None] * model_gain).astype(jnp.bfloat16).reshape(IMAGES * IMG_TOK, D)
    position = jnp.argsort(image_order).astype(jnp.int32)
    rollout_pos = position[rollout_image].reshape(GROUPS, IMGS_G * ROLL)
    rollout_pos = rollout_pos - (jnp.arange(GROUPS, dtype=jnp.int32) * IMGS_G)[:, None]
    grouped_cot = cotangent.reshape(GROUPS, IMGS_G * ROLL, IMG_TOK * D)

    def group_sum(packed):
        local_pos, cot_block = packed
        return jax.ops.segment_sum(cot_block.astype(jnp.float32), local_pos, num_segments=IMGS_G)
    summed = lax.map(group_sum, (rollout_pos, grouped_cot)).reshape(IMAGES, IMG_TOK, D)
    token_valid = jnp.arange(IMG_TOK, dtype=jnp.int32)[None, :] < counts[image_order][:, None]
    summed = summed * token_valid[..., None].astype(jnp.float32)
    inner_sum = lax.optimization_barrier(jnp.sum(summed * model_gain * hidden, axis=-1))
    token_grad = inverse[..., None] * model_gain * summed - hidden * (inverse ** 3 / D * inner_sum)[..., None]
    token_grad = token_grad.astype(jnp.bfloat16).reshape(IMAGES * IMG_TOK, D)
    merged_sorted = merged.reshape(IMAGES, IMG_TOK, DM)[image_order].reshape(IMAGES * IMG_TOK, DM)
    merger_grad = jnp.dot(merged_sorted.T, token_grad, preferred_element_type=jnp.float32)
    return (normed_tokens, merger_grad)
```

```python
import functools

import jax
import jax.numpy as jnp
from jax import lax
from jax.experimental import pallas as pl
from jax.experimental.pallas import tpu as pltpu
from jax.sharding import PartitionSpec as P

HEADS = 16
MERGE = 4
EPSILON = 1e-06
VMEM_BYTES = 48 * 1024 * 1024

F32 = jnp.float32
BF16 = jnp.bfloat16
I32 = jnp.int32


def iota(shape, dim):
    return lax.broadcasted_iota(I32, shape, dim)


def mm(a, b):
    return jnp.dot(a, b, preferred_element_type=F32)


def one_hot(condition):
    return jnp.where(condition, 1.0, 0.0).astype(BF16)


def shift_of(size):
    assert size & (size - 1) == 0
    return size.bit_length() - 1


def attention_kernel(own_image, grid_ref, q_ref, k_ref, v_ref, res_ref, out_proj_hbm, gain_ref, out_ref, proj, sem):
    load = pltpu.make_async_copy(out_proj_hbm, proj, sem)
    load.start()
    rows, width = q_ref.shape
    head = width // HEADS
    image = own_image()
    valid = MERGE * grid_ref[image, 0] * grid_ref[image, 1]
    feature = iota((1, width), 1)
    in_head = [(feature >= h * head) & (feature < (h + 1) * head) for h in range(HEADS)]
    q = q_ref[...].astype(F32)
    q_heads = jnp.concatenate([jnp.where(m, q, 0.0) for m in in_head], axis=0).astype(BF16)
    scores = lax.dot_general(
        q_heads, k_ref[...], (((1,), (1,)), ((), ())), preferred_element_type=F32
    ) * head ** (-0.5)
    scores = jnp.where(iota(scores.shape, 1) < valid, scores, -1e30)
    scores = jnp.exp(scores - jnp.max(scores, axis=1, keepdims=True))
    weights = (scores / jnp.sum(scores, axis=1, keepdims=True)).astype(BF16)
    spread = mm(weights, v_ref[...])
    attended = jnp.zeros((rows, width), F32)
    for h, m in enumerate(in_head):
        attended = attended + jnp.where(m, spread[h * rows : (h + 1) * rows], 0.0)
    load.wait()
    mixed = res_ref[...].astype(F32) + mm(attended.astype(BF16), proj[...])
    scale = lax.rsqrt(jnp.mean(mixed * mixed, axis=1, keepdims=True) + EPSILON)
    row_valid = jnp.where(iota((rows, 1), 0) < valid, 1.0, 0.0)
    out_ref[...] = (mixed * scale * gain_ref[...][None, :] * row_valid).astype(BF16)


def cotangent_kernel(dp_index, members, roll_ref, grid_ref, cot_ref, *out_refs):
    rollouts = roll_ref.shape[0]
    slots = cot_ref.shape[0] // rollouts
    bits = shift_of(slots)
    me = dp_index()
    roll = roll_ref[...][None, :]
    high, low = (roll >> 8).astype(F32), (roll & 255).astype(F32)
    pair = jnp.concatenate([high, low] + [jnp.zeros((6, rollouts), F32)], axis=0).astype(BF16)
    wide = rollouts * slots
    spread = one_hot((iota((rollouts, wide), 1) >> bits) == iota((rollouts, wide), 0))
    pair = mm(pair, spread)
    roll_wide = (pair[0:1] * 256.0 + pair[1:2]).astype(I32)
    rows = members * slots
    row, column = iota((rows, wide), 0), iota((rows, wide), 1)
    same_slot = (row & (slots - 1)) == (column & (slots - 1))
    repeat = one_hot((iota((rows, members), 0) >> bits) == iota((rows, members), 1))
    for k, out_ref in enumerate(out_refs):
        first = pl.multiple_of((me ^ k) * members, members)
        grid = grid_ref[pl.ds(first, members), :]
        count = (grid[:, 0:1] * grid[:, 1:2]).astype(F32)
        count = mm(repeat, jnp.broadcast_to(count, (members, 128)).astype(BF16))[:, 0:1]
        slot_valid = (iota((rows, 1), 0) & (slots - 1)).astype(F32) < count
        pick = (roll_wide == first + (row >> bits)) & same_slot & slot_valid
        out_ref[...] = mm(one_hot(pick), cot_ref[...]).astype(BF16)


def projection_kernel(
    indices, dp_count, mp_count, rep_count, *refs
):
    pieces = refs[:mp_count]
    sums = refs[mp_count : mp_count + dp_count]
    weight_hbm, gain_ref = refs[mp_count + dp_count : mp_count + dp_count + 2]
    outs = refs[mp_count + dp_count + 2 :]
    messages, partial_ref = outs[:dp_count], outs[dp_count]
    gathered, merged, weight, sems = outs[dp_count + 1 :]
    chunks = sems.shape[0]
    depth = weight.shape[0] // chunks
    loads = []
    for c in range(chunks):
        part = pl.ds(c * depth, depth)
        loads.append(pltpu.make_async_copy(weight_hbm.at[part, :], weight.at[part, :], sems.at[c]))
        loads[-1].start()
    dp, mp, rep = indices()
    patches = pieces[0].shape[0] // rep_count
    tokens = patches // MERGE
    width = pieces[0].shape[1]
    members = mp_count * rep_count
    for b, piece in enumerate(pieces):
        for a in range(rep_count):
            place = (mp ^ b) * rep_count + (rep ^ a)
            gathered[pl.ds(pl.multiple_of(place * patches, patches), patches), :] = piece[
                a * patches : (a + 1) * patches, :
            ]
    rows = members * tokens
    everything = members * patches
    to, source = iota((everything, everything), 0), iota((everything, everything), 1)
    within = to & (rows - 1)
    wanted = (
        ((within >> shift_of(tokens)) << shift_of(patches))
        + ((within & (tokens - 1)) << shift_of(MERGE))
        + (to >> shift_of(rows))
    )
    merged[...] = mm(one_hot(wanted == source), gathered[...]).astype(BF16)
    columns = weight.shape[1]
    total = jnp.zeros((rows, columns), F32)
    for c in range(chunks):
        loads[c].wait()
        j, at = divmod(c * depth, width)
        total = total + mm(merged[j * rows : (j + 1) * rows, at : at + depth], weight[c * depth : (c + 1) * depth, :])
    hidden = total.astype(BF16)
    summed = sums[0][...].astype(F32)
    for other in sums[1:]:
        summed = summed + other[...].astype(F32)
    wide = hidden.astype(F32)
    squares = jnp.sum(wide * wide, axis=1, keepdims=True)
    inner = jnp.sum(summed * gain_ref[...][None, :] * wide, axis=1, keepdims=True)
    diagonal = iota((rows, rows), 0) == iota((rows, rows), 1)
    both = jnp.concatenate(
        [jnp.sum(jnp.where(diagonal, x, 0.0), axis=0, keepdims=True) for x in (squares, inner)], axis=0
    )
    partial_ref[...] = jnp.broadcast_to(both[None], partial_ref.shape)
    summed = summed.astype(BF16)
    share = MERGE * width // dp_count
    per_patch = width // share
    for k, message in enumerate(messages):
        message[:, 0:columns] = hidden
        message[:, columns : 2 * columns] = summed
        target = dp ^ k
        first = pl.multiple_of((target >> shift_of(per_patch)) * rows, rows)
        for q in range(per_patch):

            @pl.when((target & (per_patch - 1)) == q)
            def _():
                message[:, 2 * columns : 2 * columns + share] = merged[
                    pl.ds(first, rows), q * share : (q + 1) * share
                ]


def final_kernel(dp_index, dp_count, model_width, *refs):
    messages = refs[:dp_count]
    partial_ref, gain_ref, group_ref = refs[dp_count : dp_count + 3]
    normed_ref, grad_hbm, token_grad, normed, merged, grad, sems = refs[dp_count + 3 :]
    me = dp_index()
    rows, columns = normed_ref.shape
    members = partial_ref.shape[0] // dp_count
    share = merged.shape[1]
    tokens = rows // members
    gain = gain_ref[...][None, :]
    diagonal = iota((rows, rows), 0) == iota((rows, rows), 1)
    for k, message in enumerate(messages):
        both = jnp.sum(partial_ref[pl.ds(pl.multiple_of((me ^ k) * members, members), members)], axis=0)
        inverse = lax.rsqrt(both[0:1] / model_width + EPSILON)
        factor = inverse * inverse * inverse / model_width * both[1:2]
        inverse, factor = (
            jnp.sum(jnp.where(diagonal, x, 0.0), axis=1, keepdims=True) for x in (inverse, factor)
        )
        hidden = message[:, 0:columns].astype(F32)
        summed = message[:, columns : 2 * columns].astype(F32)
        block = slice(k * rows, (k + 1) * rows)
        normed[block, :] = (hidden * inverse * gain).astype(BF16)
        token_grad[block, :] = (inverse * gain * summed - hidden * factor).astype(BF16)
        merged[block, :] = message[:, 2 * columns : 2 * columns + share]
    copies = []
    chunk = min(share, 256)
    for c, at in enumerate(range(0, share, chunk)):
        size = min(chunk, share - at)
        grad[at : at + size, :] = lax.dot_general(
            merged[:, at : at + size], token_grad[...], (((0,), (0,)), ((), ())), preferred_element_type=F32
        )
        copies.append(pltpu.make_async_copy(grad.at[pl.ds(at, size), :], grad_hbm.at[pl.ds(at, size), :], sems.at[c]))
        copies[-1].start()
    images = group_ref.shape[0]
    mine = group_ref[...][None, :] == me
    ours = jnp.broadcast_to(jnp.where(mine, 1.0, 0.0), (8, images)).astype(BF16)
    rank = mm(ours, one_hot(iota((images, images), 0) < iota((images, images), 1)))
    slot = jnp.where(mine, rank, -1.0).astype(BF16)
    column = iota((images, dp_count * rows), 1)
    image = ((me ^ (column >> shift_of(rows))) << shift_of(members)) + (
        (column >> shift_of(tokens)) & (members - 1)
    )
    slot = mm(slot, one_hot(image == iota((images, dp_count * rows), 0)))[0:1]
    row, column = iota((rows, dp_count * rows), 0), iota((rows, dp_count * rows), 1)
    pick = (slot == (row >> shift_of(tokens)).astype(F32)) & ((row & (tokens - 1)) == (column & (tokens - 1)))
    normed_ref[...] = mm(one_hot(pick), normed[...]).astype(BF16)
    for copy in copies:
        copy.wait()


def swaps(axis, size, k):
    return [(i, i ^ k) for i in range(size)]


def on_device(
    query_rows,
    key_rows,
    value_rows,
    residual,
    out_proj,
    merge_gain,
    merger_proj,
    model_gain,
    image_grid,
    image_group,
    rollout_image,
    cotangent,
):
    dp_count, mp_count, rep_count = (lax.axis_size(a) for a in ("dp", "mp", "rep"))
    members = mp_count * rep_count
    patches, width = query_rows.shape
    tokens = patches // MERGE
    rows = members * tokens
    columns = merger_proj.shape[1]
    share = MERGE * width // dp_count
    devices = dp_count * members
    vmem, smem, hbm = (
        pl.BlockSpec(memory_space=m) for m in (pltpu.VMEM, pltpu.SMEM, pl.ANY)
    )
    params = pltpu.CompilerParams(vmem_limit_bytes=VMEM_BYTES)
    own_image = lambda: lax.axis_index(("dp", "mp", "rep"))
    dp_index = lambda: lax.axis_index("dp")
    indices = lambda: (lax.axis_index("dp"), lax.axis_index("mp"), lax.axis_index("rep"))
    shape = jax.ShapeDtypeStruct

    merged = pl.pallas_call(
        functools.partial(attention_kernel, own_image),
        out_shape=shape((patches, width), BF16),
        in_specs=[smem, vmem, vmem, vmem, vmem, hbm, vmem],
        out_specs=vmem,
        scratch_shapes=[pltpu.VMEM((width, width), BF16), pltpu.SemaphoreType.DMA],
        compiler_params=params,
        name="attention",
    )(image_grid, query_rows, key_rows, value_rows, residual, out_proj, merge_gain)

    sums = pl.pallas_call(
        functools.partial(cotangent_kernel, dp_index, members),
        out_shape=[shape((rows, columns), BF16)] * dp_count,
        in_specs=[vmem, vmem, vmem],
        out_specs=[vmem] * dp_count,
        compiler_params=params,
        name="cotangent_sums",
    )(rollout_image, image_grid, cotangent)

    pair = jnp.concatenate(
        [merged] + [lax.ppermute(merged, "rep", swaps("rep", rep_count, a)) for a in range(1, rep_count)], axis=0
    )
    pieces = [pair] + [lax.ppermute(pair, "mp", swaps("mp", mp_count, b)) for b in range(1, mp_count)]
    sums = [sums[0]] + [lax.ppermute(sums[k], "dp", swaps("dp", dp_count, k)) for k in range(1, dp_count)]

    chunks = 8
    *messages, partial = pl.pallas_call(
        functools.partial(projection_kernel, indices, dp_count, mp_count, rep_count),
        out_shape=[shape((rows, 2 * columns + share), BF16)] * dp_count + [shape((devices, 2, rows), F32)],
        in_specs=[vmem] * (mp_count + dp_count) + [hbm, vmem],
        out_specs=[vmem] * (dp_count + 1),
        scratch_shapes=[
            pltpu.VMEM((members * patches, width), BF16),
            pltpu.VMEM((members * patches, width), BF16),
            pltpu.VMEM(merger_proj.shape, BF16),
            pltpu.SemaphoreType.DMA((chunks,)),
        ],
        compiler_params=params,
        name="projection",
    )(*pieces, *sums, merger_proj, model_gain)

    messages = [messages[0]] + [
        lax.ppermute(messages[k], "dp", swaps("dp", dp_count, k)) for k in range(1, dp_count)
    ]
    partial = lax.all_to_all(partial, ("dp", "mp", "rep"), split_axis=0, concat_axis=0, tiled=True)

    normed_tokens, merger_grad = pl.pallas_call(
        functools.partial(final_kernel, dp_index, dp_count, float(columns * members)),
        out_shape=[shape((rows, columns), BF16), shape((share, columns), F32)],
        in_specs=[vmem] * (dp_count + 3),
        out_specs=[vmem, hbm],
        scratch_shapes=[
            pltpu.VMEM((dp_count * rows, columns), BF16),
            pltpu.VMEM((dp_count * rows, columns), BF16),
            pltpu.VMEM((dp_count * rows, share), BF16),
            pltpu.VMEM((share, columns), F32),
            pltpu.SemaphoreType.DMA((-(-share // 256),)),
        ],
        compiler_params=params,
        name="final",
    )(*messages, partial, model_gain, image_group)
    return normed_tokens, merger_grad


def solution(mesh):
    return jax.shard_map(
        on_device,
        mesh=mesh,
        in_specs=(
            P(("dp", "mp", "rep"), None),
            P(("dp", "mp", "rep"), None),
            P(("dp", "mp", "rep"), None),
            P(("dp", "mp", "rep"), None),
            P(),
            P(),
            P(None, ("mp", "rep")),
            P(("mp", "rep")),
            P(),
            P(),
            P("dp"),
            P("dp", ("mp", "rep")),
        ),
        out_specs=(P("dp", ("mp", "rep")), P("dp", ("mp", "rep"))),
        check_vma=False,
    )
```

```python
import functools

import jax
import jax.numpy as jnp
from jax import lax
from jax.experimental import pallas as pl
from jax.experimental.pallas import tpu as pltpu
from jax.sharding import PartitionSpec as P

HEADS = 16
MERGE = 4
EPSILON = 1e-06
VMEM_BYTES = 24 * 1024 * 1024

F32 = jnp.float32
BF16 = jnp.bfloat16
I32 = jnp.int32


def iota(shape, dim):
    return lax.broadcasted_iota(I32, shape, dim)


def mm(a, b):
    return jnp.dot(a, b, preferred_element_type=F32)


def one_hot(condition):
    return jnp.where(condition, 1.0, 0.0).astype(BF16)


def shift_of(size):
    assert size & (size - 1) == 0
    return size.bit_length() - 1


def attention_kernel(
    own_image, grid_hbm, q_hbm, k_hbm, v_hbm, res_hbm, out_proj_hbm, gain_hbm, out_ref,
    grid_ref, q_ref, k_ref, v_ref, res_ref, proj, gain_ref, sems,
):
    pairs = [
        (q_hbm, q_ref), (k_hbm, k_ref), (grid_hbm, grid_ref), (v_hbm, v_ref),
        (out_proj_hbm, proj), (res_hbm, res_ref), (gain_hbm, gain_ref),
    ]
    loads = [pltpu.make_async_copy(source, to, sems.at[i]) for i, (source, to) in enumerate(pairs)]
    for load in loads:
        load.start()
    rows, width = q_ref.shape
    head = width // HEADS
    image = own_image()
    feature = iota((1, width), 1)
    in_head = [(feature >= h * head) & (feature < (h + 1) * head) for h in range(HEADS)]
    loads[0].wait()
    q = q_ref[...].astype(F32)
    q_heads = jnp.concatenate([jnp.where(m, q, 0.0) for m in in_head], axis=0).astype(BF16)
    loads[1].wait()
    scores = lax.dot_general(
        q_heads, k_ref[...], (((1,), (1,)), ((), ())), preferred_element_type=F32
    ) * head ** (-0.5)
    loads[2].wait()
    counts = grid_ref[0:1, :] * grid_ref[1:2, :]
    valid = MERGE * jnp.sum(jnp.where(iota(counts.shape, 1) == image, counts, 0), axis=1, keepdims=True)
    scores = jnp.where(iota(scores.shape, 1) < valid, scores, -1e30)
    scores = jnp.exp(scores - jnp.max(scores, axis=1, keepdims=True))
    weights = (scores / jnp.sum(scores, axis=1, keepdims=True)).astype(BF16)
    loads[3].wait()
    spread = mm(weights, v_ref[...])
    attended = jnp.zeros((rows, width), F32)
    for h, m in enumerate(in_head):
        attended = attended + jnp.where(m, spread[h * rows : (h + 1) * rows], 0.0)
    loads[4].wait()
    mixed = mm(attended.astype(BF16), proj[...])
    loads[5].wait()
    mixed = res_ref[...].astype(F32) + mixed
    scale = lax.rsqrt(jnp.mean(mixed * mixed, axis=1, keepdims=True) + EPSILON)
    row_valid = jnp.where(iota((rows, 1), 0) < valid, 1.0, 0.0)
    loads[6].wait()
    out_ref[...] = (mixed * scale * gain_ref[...][None, :] * row_valid).astype(BF16)


def cotangent_kernel(dp_index, members, roll_hbm, grid_hbm, cot_hbm, *refs):
    out_refs = refs[:-4]
    roll_ref, grid_ref, cot_ref, sems = refs[-4:]
    pairs = [(roll_hbm, roll_ref), (grid_hbm, grid_ref), (cot_hbm, cot_ref)]
    loads = [pltpu.make_async_copy(source, to, sems.at[i]) for i, (source, to) in enumerate(pairs)]
    for load in loads:
        load.start()
    loads[0].wait()
    rollouts = roll_ref.shape[0]
    slots = cot_ref.shape[0] // rollouts
    bits = shift_of(slots)
    me = dp_index()
    roll = roll_ref[...][None, :]
    high, low = (roll >> 8).astype(F32), (roll & 255).astype(F32)
    pair = jnp.concatenate([high, low] + [jnp.zeros((6, rollouts), F32)], axis=0).astype(BF16)
    wide = rollouts * slots
    spread = one_hot((iota((rollouts, wide), 1) >> bits) == iota((rollouts, wide), 0))
    pair = mm(pair, spread)
    roll_wide = (pair[0:1] * 256.0 + pair[1:2]).astype(I32)
    rows = members * slots
    row, column = iota((rows, wide), 0), iota((rows, wide), 1)
    same_slot = (row & (slots - 1)) == (column & (slots - 1))
    loads[1].wait()
    counts = grid_ref[0:1, :] * grid_ref[1:2, :]
    images = counts.shape[1]
    image, own_row = iota((rows, images), 1), iota((rows, 1), 0)
    loads[2].wait()
    for k, out_ref in enumerate(out_refs):
        first = (me ^ k) * members
        count = jnp.sum(jnp.where(image == first + (own_row >> bits), counts, 0), axis=1, keepdims=True)
        pick = (roll_wide == first + (row >> bits)) & same_slot & ((own_row & (slots - 1)) < count)
        out_ref[...] = mm(one_hot(pick), cot_ref[...]).astype(BF16)


def prefetch_kernel(after_ref, *refs):
    del after_ref
    count = len(refs) // 2
    loads = [pltpu.make_async_copy(refs[i], refs[count + i], refs[-1].at[i]) for i in range(count)]
    for load in loads:
        load.start()
    for load in loads:
        load.wait()


def projection_kernel(indices, dp_count, mp_count, rep_count, *refs):
    pieces = refs[:mp_count]
    sums = refs[mp_count : mp_count + dp_count]
    weight, gain_ref = refs[mp_count + dp_count : mp_count + dp_count + 2]
    outs = refs[mp_count + dp_count + 2 :]
    messages, partial_ref = outs[:dp_count], outs[dp_count]
    gathered, merged = outs[dp_count + 1 :]
    dp, mp, rep = indices()
    patches = pieces[0].shape[0] // rep_count
    tokens = patches // MERGE
    width = pieces[0].shape[1]
    members = mp_count * rep_count
    for b, piece in enumerate(pieces):
        for a in range(rep_count):
            place = (mp ^ b) * rep_count + (rep ^ a)
            gathered[pl.ds(pl.multiple_of(place * patches, patches), patches), :] = piece[
                a * patches : (a + 1) * patches, :
            ]
    rows = members * tokens
    everything = members * patches
    to, source = iota((everything, everything), 0), iota((everything, everything), 1)
    within = to & (rows - 1)
    wanted = (
        ((within >> shift_of(tokens)) << shift_of(patches))
        + ((within & (tokens - 1)) << shift_of(MERGE))
        + (to >> shift_of(rows))
    )
    merged[...] = mm(one_hot(wanted == source), gathered[...]).astype(BF16)
    columns = weight.shape[1]
    total = jnp.zeros((rows, columns), F32)
    for j in range(MERGE):
        total = total + mm(merged[j * rows : (j + 1) * rows, :], weight[j * width : (j + 1) * width, :])
    hidden = total.astype(BF16)
    summed = sums[0][...].astype(F32)
    for other in sums[1:]:
        summed = summed + other[...].astype(F32)
    wide = hidden.astype(F32)
    squares = jnp.sum(wide * wide, axis=1, keepdims=True)
    inner = jnp.sum(summed * gain_ref[...][None, :] * wide, axis=1, keepdims=True)
    diagonal = iota((rows, rows), 0) == iota((rows, rows), 1)
    both = jnp.concatenate(
        [jnp.sum(jnp.where(diagonal, x, 0.0), axis=0, keepdims=True) for x in (squares, inner)], axis=0
    )
    partial_ref[...] = jnp.broadcast_to(both[None], partial_ref.shape)
    summed = summed.astype(BF16)
    share = MERGE * width // dp_count
    per_patch = width // share
    for k, message in enumerate(messages):
        message[:, 0:columns] = hidden
        message[:, columns : 2 * columns] = summed
        target = dp ^ k
        first = pl.multiple_of((target >> shift_of(per_patch)) * rows, rows)
        for q in range(per_patch):

            @pl.when((target & (per_patch - 1)) == q)
            def _():
                message[:, 2 * columns : 2 * columns + share] = merged[
                    pl.ds(first, rows), q * share : (q + 1) * share
                ]


def final_kernel(dp_index, dp_count, model_width, *refs):
    messages = refs[:dp_count]
    partial_ref, gain_ref, group_ref = refs[dp_count : dp_count + 3]
    normed_ref, grad_hbm, token_grad, normed, merged, grad, sems = refs[dp_count + 3 :]
    me = dp_index()
    rows, columns = normed_ref.shape
    members = partial_ref.shape[0] // dp_count
    share = merged.shape[1]
    tokens = rows // members
    gain = gain_ref[...][None, :]
    diagonal = iota((rows, rows), 0) == iota((rows, rows), 1)
    for k, message in enumerate(messages):
        both = jnp.sum(partial_ref[pl.ds(pl.multiple_of((me ^ k) * members, members), members)], axis=0)
        inverse = lax.rsqrt(both[0:1] / model_width + EPSILON)
        factor = inverse * inverse * inverse / model_width * both[1:2]
        inverse, factor = (
            jnp.sum(jnp.where(diagonal, x, 0.0), axis=1, keepdims=True) for x in (inverse, factor)
        )
        hidden = message[:, 0:columns].astype(F32)
        summed = message[:, columns : 2 * columns].astype(F32)
        block = slice(k * rows, (k + 1) * rows)
        normed[block, :] = (hidden * inverse * gain).astype(BF16)
        token_grad[block, :] = (inverse * gain * summed - hidden * factor).astype(BF16)
        merged[block, :] = message[:, 2 * columns : 2 * columns + share]
    copies = []
    chunk = min(share, 256)
    for c, at in enumerate(range(0, share, chunk)):
        size = min(chunk, share - at)
        grad[at : at + size, :] = lax.dot_general(
            merged[:, at : at + size], token_grad[...], (((0,), (0,)), ((), ())), preferred_element_type=F32
        )
        copies.append(pltpu.make_async_copy(grad.at[pl.ds(at, size), :], grad_hbm.at[pl.ds(at, size), :], sems.at[c]))
        copies[-1].start()
    images = group_ref.shape[0]
    mine = group_ref[...][None, :] == me
    ours = jnp.broadcast_to(jnp.where(mine, 1.0, 0.0), (8, images)).astype(BF16)
    rank = mm(ours, one_hot(iota((images, images), 0) < iota((images, images), 1)))
    slot = jnp.where(mine, rank, -1.0).astype(BF16)
    column = iota((images, dp_count * rows), 1)
    image = ((me ^ (column >> shift_of(rows))) << shift_of(members)) + (
        (column >> shift_of(tokens)) & (members - 1)
    )
    slot = mm(slot, one_hot(image == iota((images, dp_count * rows), 0)))[0:1]
    row, column = iota((rows, dp_count * rows), 0), iota((rows, dp_count * rows), 1)
    pick = (slot == (row >> shift_of(tokens)).astype(F32)) & ((row & (tokens - 1)) == (column & (tokens - 1)))
    normed_ref[...] = mm(one_hot(pick), normed[...]).astype(BF16)
    for copy in copies:
        copy.wait()


def swaps(axis, size, k):
    return [(i, i ^ k) for i in range(size)]


def on_device(
    query_rows,
    key_rows,
    value_rows,
    residual,
    out_proj,
    merge_gain,
    merger_proj,
    model_gain,
    image_grid,
    image_group,
    rollout_image,
    cotangent,
):
    dp_count, mp_count, rep_count = (lax.axis_size(a) for a in ("dp", "mp", "rep"))
    members = mp_count * rep_count
    patches, width = query_rows.shape
    tokens = patches // MERGE
    rows = members * tokens
    columns = merger_proj.shape[1]
    share = MERGE * width // dp_count
    devices = dp_count * members
    vmem, hbm = (pl.BlockSpec(memory_space=m) for m in (pltpu.VMEM, pltpu.HBM))
    scratch, dma = pltpu.VMEM, pltpu.SemaphoreType.DMA
    params = pltpu.CompilerParams(vmem_limit_bytes=VMEM_BYTES)
    stay = lambda *arrays: [pltpu.with_memory_space_constraint(x, pltpu.HBM) for x in arrays]
    grid = image_grid.T
    own_image = lambda: lax.axis_index(("dp", "mp", "rep"))
    dp_index = lambda: lax.axis_index("dp")
    indices = lambda: (lax.axis_index("dp"), lax.axis_index("mp"), lax.axis_index("rep"))
    shape = jax.ShapeDtypeStruct

    merged = pl.pallas_call(
        functools.partial(attention_kernel, own_image),
        out_shape=shape((patches, width), BF16),
        in_specs=[hbm] * 7,
        out_specs=vmem,
        scratch_shapes=[scratch(grid.shape, I32)]
        + [scratch((patches, width), BF16)] * 4
        + [scratch((width, width), BF16), scratch((width,), F32), dma((7,))],
        compiler_params=params,
        name="attention",
    )(*stay(grid, query_rows, key_rows, value_rows, residual, out_proj, merge_gain))

    sums = pl.pallas_call(
        functools.partial(cotangent_kernel, dp_index, members),
        out_shape=[shape((rows, columns), BF16)] * dp_count,
        in_specs=[hbm] * 3,
        out_specs=[vmem] * dp_count,
        scratch_shapes=[
            scratch(rollout_image.shape, I32), scratch(grid.shape, I32), scratch(cotangent.shape, BF16), dma((3,))
        ],
        compiler_params=params,
        name="cotangent_sums",
    )(*stay(rollout_image, grid, cotangent))

    pair = jnp.concatenate(
        [merged] + [lax.ppermute(merged, "rep", swaps("rep", rep_count, a)) for a in range(1, rep_count)], axis=0
    )
    pieces = [pair] + [lax.ppermute(pair, "mp", swaps("mp", mp_count, b)) for b in range(1, mp_count)]
    sums = [sums[0]] + [lax.ppermute(sums[k], "dp", swaps("dp", dp_count, k)) for k in range(1, dp_count)]

    early = (merger_proj, model_gain, image_group)
    weight, gain, group = pl.pallas_call(
        prefetch_kernel,
        out_shape=[pltpu.VMEM(x.shape, x.dtype) for x in early],
        in_specs=[pl.BlockSpec(memory_space=pl.ANY)] + [hbm] * 3,
        out_specs=[vmem] * 3,
        scratch_shapes=[dma((3,))],
        compiler_params=params,
        cost_estimate=pl.CostEstimate(flops=0, bytes_accessed=2 * merger_proj.size, transcendentals=0),
        name="prefetch",
    )(pair, *stay(*early))

    *messages, partial = pl.pallas_call(
        functools.partial(projection_kernel, indices, dp_count, mp_count, rep_count),
        out_shape=[shape((rows, 2 * columns + share), BF16)] * dp_count + [shape((devices, 2, rows), F32)],
        in_specs=[vmem] * (mp_count + dp_count + 2),
        out_specs=[vmem] * (dp_count + 1),
        scratch_shapes=[
            scratch((members * patches, width), BF16),
            scratch((members * patches, width), BF16),
        ],
        compiler_params=params,
        name="projection",
    )(*pieces, *sums, weight, gain)

    messages = [messages[0]] + [
        lax.ppermute(messages[k], "dp", swaps("dp", dp_count, k)) for k in range(1, dp_count)
    ]
    partial = lax.all_to_all(partial, ("dp", "mp", "rep"), split_axis=0, concat_axis=0, tiled=True)

    normed_tokens, merger_grad = pl.pallas_call(
        functools.partial(final_kernel, dp_index, dp_count, float(columns * members)),
        out_shape=[shape((rows, columns), BF16), shape((share, columns), F32)],
        in_specs=[vmem] * (dp_count + 3),
        out_specs=[vmem, hbm],
        scratch_shapes=[
            scratch((dp_count * rows, columns), BF16),
            scratch((dp_count * rows, columns), BF16),
            scratch((dp_count * rows, share), BF16),
            scratch((share, columns), F32),
            dma((-(-share // 256),)),
        ],
        compiler_params=params,
        name="final",
    )(*messages, partial, gain, group)
    return normed_tokens, merger_grad


def solution(mesh):
    return jax.shard_map(
        on_device,
        mesh=mesh,
        in_specs=(
            P(("dp", "mp", "rep"), None),
            P(("dp", "mp", "rep"), None),
            P(("dp", "mp", "rep"), None),
            P(("dp", "mp", "rep"), None),
            P(),
            P(),
            P(None, ("mp", "rep")),
            P(("mp", "rep")),
            P(),
            P(),
            P("dp"),
            P("dp", ("mp", "rep")),
        ),
        out_specs=(P("dp", ("mp", "rep")), P("dp", ("mp", "rep"))),
        check_vma=False,
    )
```

```python
import functools

import jax
import jax.numpy as jnp
from jax import lax
from jax.experimental import pallas as pl
from jax.experimental.pallas import tpu as pltpu
from jax.sharding import PartitionSpec as P

HEADS = 16
MERGE = 4
EPSILON = 1e-06
VMEM_BYTES = 24 * 1024 * 1024

F32 = jnp.float32
BF16 = jnp.bfloat16
I32 = jnp.int32


def iota(shape, dim):
    return lax.broadcasted_iota(I32, shape, dim)


def mm(a, b):
    return jnp.dot(a, b, preferred_element_type=F32)


def one_hot(condition):
    return jnp.where(condition, 1.0, 0.0).astype(BF16)


def shift_of(size):
    assert size & (size - 1) == 0
    return size.bit_length() - 1


def attention_kernel(
    own_image, grid_hbm, q_hbm, k_hbm, v_hbm, res_hbm, out_proj_hbm, gain_hbm, out_ref,
    grid_ref, q_ref, k_ref, v_ref, res_ref, proj, gain_ref, sems,
):
    pairs = [
        (q_hbm, q_ref), (k_hbm, k_ref), (grid_hbm, grid_ref), (v_hbm, v_ref),
        (out_proj_hbm, proj), (res_hbm, res_ref), (gain_hbm, gain_ref),
    ]
    loads = start_all(pairs, sems)
    rows, width = q_ref.shape
    head = width // HEADS
    image = own_image()
    feature = iota((1, width), 1)
    in_head = [(feature >= h * head) & (feature < (h + 1) * head) for h in range(HEADS)]
    loads[0].wait()
    q = q_ref[...].astype(F32)
    q_heads = jnp.concatenate([jnp.where(m, q, 0.0) for m in in_head], axis=0).astype(BF16)
    loads[1].wait()
    scores = lax.dot_general(
        q_heads, k_ref[...], (((1,), (1,)), ((), ())), preferred_element_type=F32
    ) * head ** (-0.5)
    loads[2].wait()
    counts = grid_ref[0:1, :] * grid_ref[1:2, :]
    valid = MERGE * jnp.sum(jnp.where(iota(counts.shape, 1) == image, counts, 0), axis=1, keepdims=True)
    scores = jnp.where(iota(scores.shape, 1) < valid, scores, -1e30)
    scores = jnp.exp(scores - jnp.max(scores, axis=1, keepdims=True))
    weights = (scores / jnp.sum(scores, axis=1, keepdims=True)).astype(BF16)
    loads[3].wait()
    spread = mm(weights, v_ref[...])
    attended = jnp.zeros((rows, width), F32)
    for h, m in enumerate(in_head):
        attended = attended + jnp.where(m, spread[h * rows : (h + 1) * rows], 0.0)
    loads[4].wait()
    mixed = mm(attended.astype(BF16), proj[...])
    loads[5].wait()
    mixed = res_ref[...].astype(F32) + mixed
    scale = lax.rsqrt(jnp.mean(mixed * mixed, axis=1, keepdims=True) + EPSILON)
    row_valid = jnp.where(iota((rows, 1), 0) < valid, 1.0, 0.0)
    loads[6].wait()
    out_ref[...] = (mixed * scale * gain_ref[...][None, :] * row_valid).astype(BF16)


def start_all(pairs, sems):
    loads = [pltpu.make_async_copy(source, to, sems.at[i]) for i, (source, to) in enumerate(pairs)]
    for load in loads:
        load.start()
    return loads


def cotangent_kernel(dp_index, members, roll_hbm, grid_hbm, group_hbm, cot_hbm, weight_hbm, *refs):
    out_ref, place_ref, weight_ref, roll_ref, grid_ref, group_ref, cot_ref, sems = refs
    first_part = weight_hbm.at[pl.ds(0, weight_ref.shape[0]), :]
    loads = start_all(
        [
            (group_hbm, group_ref), (roll_hbm, roll_ref), (grid_hbm, grid_ref), (cot_hbm, cot_ref),
            (first_part, weight_ref),
        ],
        sems,
    )
    me = dp_index()
    rollouts = roll_ref.shape[0]
    slots = cot_ref.shape[0] // rollouts
    bits = shift_of(slots)
    wide = rollouts * slots
    rows = members * slots
    spread = one_hot((iota((rollouts, wide), 1) >> bits) == iota((rollouts, wide), 0))
    loads[0].wait()
    group = group_ref[...][None, :]
    images = group.shape[1]
    square = (images, images)
    column = jnp.sum(jnp.where(iota(square, 0) == iota(square, 1), group, 0), axis=1, keepdims=True)
    earlier = (column == group) & (iota(square, 0) < iota(square, 1))
    place = group * members + jnp.sum(jnp.where(earlier, 1, 0), axis=0, keepdims=True)
    place_ref[...] = place
    own_row = iota((rows, 1), 0)
    ours = place == me * members + (own_row >> bits)
    image = jnp.sum(jnp.where(ours, iota((rows, images), 1), 0), axis=1, keepdims=True)
    loads[1].wait()
    roll = roll_ref[...][None, :]
    high, low = (roll >> 8).astype(F32), (roll & 255).astype(F32)
    pair = jnp.concatenate([high, low] + [jnp.zeros((6, rollouts), F32)], axis=0).astype(BF16)
    pair = mm(pair, spread)
    roll_wide = (pair[0:1] * 256.0 + pair[1:2]).astype(I32)
    loads[2].wait()
    count = jnp.sum(jnp.where(ours, grid_ref[0:1, :] * grid_ref[1:2, :], 0), axis=1, keepdims=True)
    slot = own_row & (slots - 1)
    pick = (roll_wide == image) & (slot == (iota((1, wide), 1) & (slots - 1))) & (slot < count)
    loads[3].wait()
    out_ref[...] = mm(one_hot(pick), cot_ref[...]).astype(BF16)
    loads[4].wait()


def prefetch_kernel(after_ref, weight_hbm, gain_hbm, *refs):
    del after_ref
    sums = refs[:-4]
    weight_ref, gain_ref, joined_ref, sems = refs[-4:]
    part = weight_ref.shape[0]
    second = weight_hbm.at[pl.ds(weight_hbm.shape[0] - part, part), :]
    loads = start_all([(second, weight_ref), (gain_hbm, gain_ref)], sems)
    rows = sums[0].shape[0]
    for i, block in enumerate(sums):
        joined_ref[i * rows : (i + 1) * rows, :] = block[...]
    for load in loads:
        load.wait()


def collect_sums(me, dp_count, halves, everything):
    cores = len(halves)
    rows = everything.shape[0] // dp_count
    for c, half in enumerate(halves):
        for a in range(dp_count // cores):
            at = pl.multiple_of((me ^ (cores * a) ^ c) * rows, rows)
            everything[pl.ds(at, rows), :] = half[a * rows : (a + 1) * rows, :]


def pick_sums(place, first, rows, tokens, everything):
    images = place.shape[1]
    bits = shift_of(tokens)
    own_row = iota((rows, 1), 0)
    own = jnp.where(iota((rows, images), 1) == first + (own_row >> bits), place, 0)
    own = jnp.sum(own, axis=1, keepdims=True)
    column = iota((1, everything.shape[0]), 1)
    pick = (own == (column >> bits)) & ((own_row & (tokens - 1)) == (column & (tokens - 1)))
    return mm(one_hot(pick), everything[...])


def projection_kernel(indices, dp_count, mp_count, rep_count, *refs):
    pieces = refs[:mp_count]
    first_half, second_half, weight_a, weight_b, gain_ref, place_ref = refs[mp_count : mp_count + 6]
    outs = refs[mp_count + 6 :]
    messages, partial_ref = outs[:dp_count], outs[dp_count]
    gathered, merged, sums = outs[dp_count + 1 :]
    dp, mp, rep = indices()
    patches = pieces[0].shape[0] // rep_count
    tokens = patches // MERGE
    width = pieces[0].shape[1]
    members = mp_count * rep_count
    for b, piece in enumerate(pieces):
        for a in range(rep_count):
            place = (mp ^ b) * rep_count + (rep ^ a)
            gathered[pl.ds(pl.multiple_of(place * patches, patches), patches), :] = piece[
                a * patches : (a + 1) * patches, :
            ]
    rows = members * tokens
    everything = members * patches
    to, source = iota((everything, everything), 0), iota((everything, everything), 1)
    within = to & (rows - 1)
    wanted = (
        ((within >> shift_of(tokens)) << shift_of(patches))
        + ((within & (tokens - 1)) << shift_of(MERGE))
        + (to >> shift_of(rows))
    )
    merged[...] = mm(one_hot(wanted == source), gathered[...]).astype(BF16)
    columns = weight_a.shape[1]
    total = jnp.zeros((rows, columns), F32)
    for j in range(MERGE):
        weight, at = (weight_a, j) if j < MERGE // 2 else (weight_b, j - MERGE // 2)
        total = total + mm(merged[j * rows : (j + 1) * rows, :], weight[at * width : (at + 1) * width, :])
    hidden = total.astype(BF16)
    collect_sums(dp, dp_count, (first_half, second_half), sums)
    summed = pick_sums(place_ref[...], dp * members, rows, tokens, sums)
    wide = hidden.astype(F32)
    squares = jnp.sum(wide * wide, axis=1, keepdims=True)
    inner = jnp.sum(summed * gain_ref[...][None, :] * wide, axis=1, keepdims=True)
    diagonal = iota((rows, rows), 0) == iota((rows, rows), 1)
    both = jnp.concatenate(
        [jnp.sum(jnp.where(diagonal, x, 0.0), axis=0, keepdims=True) for x in (squares, inner)], axis=0
    )
    partial_ref[...] = jnp.broadcast_to(both[None], partial_ref.shape)
    share = MERGE * width // dp_count
    per_patch = width // share
    for k, message in enumerate(messages):
        message[:, 0:columns] = hidden
        target = dp ^ k
        first = pl.multiple_of((target >> shift_of(per_patch)) * rows, rows)
        for q in range(per_patch):

            @pl.when((target & (per_patch - 1)) == q)
            def _():
                message[:, columns : columns + share] = merged[
                    pl.ds(first, rows), q * share : (q + 1) * share
                ]


def final_kernel(dp_index, dp_count, model_width, *refs):
    messages = refs[:dp_count]
    partial_ref, gain_ref, place_ref, first_half, second_half = refs[dp_count : dp_count + 5]
    normed_ref, grad_hbm, token_grad, normed, merged, grad, sums, sems = refs[dp_count + 5 :]
    me = dp_index()
    rows, columns = normed_ref.shape
    members = partial_ref.shape[0] // dp_count
    share = merged.shape[1]
    tokens = rows // members
    gain = gain_ref[...][None, :]
    place = place_ref[...]
    collect_sums(me, dp_count, (first_half, second_half), sums)
    diagonal = iota((rows, rows), 0) == iota((rows, rows), 1)
    for k, message in enumerate(messages):
        both = jnp.sum(partial_ref[pl.ds(pl.multiple_of((me ^ k) * members, members), members)], axis=0)
        inverse = lax.rsqrt(both[0:1] / model_width + EPSILON)
        factor = inverse * inverse * inverse / model_width * both[1:2]
        inverse, factor = (
            jnp.sum(jnp.where(diagonal, x, 0.0), axis=1, keepdims=True) for x in (inverse, factor)
        )
        hidden = message[:, 0:columns].astype(F32)
        summed = pick_sums(place, (me ^ k) * members, rows, tokens, sums)
        block = slice(k * rows, (k + 1) * rows)
        normed[block, :] = (hidden * inverse * gain).astype(BF16)
        token_grad[block, :] = (inverse * gain * summed - hidden * factor).astype(BF16)
        merged[block, :] = message[:, columns : columns + share]
    copies = []
    chunk = min(share, 256)
    for c, at in enumerate(range(0, share, chunk)):
        size = min(chunk, share - at)
        grad[at : at + size, :] = lax.dot_general(
            merged[:, at : at + size], token_grad[...], (((0,), (0,)), ((), ())), preferred_element_type=F32
        )
        copies.append(pltpu.make_async_copy(grad.at[pl.ds(at, size), :], grad_hbm.at[pl.ds(at, size), :], sems.at[c]))
        copies[-1].start()
    images = place.shape[1]
    slot = jnp.broadcast_to(place - me * members, (8, images))
    slot = jnp.where((slot >= 0) & (slot < members), slot, -1).astype(F32).astype(BF16)
    column = iota((images, dp_count * rows), 1)
    image = ((me ^ (column >> shift_of(rows))) << shift_of(members)) + (
        (column >> shift_of(tokens)) & (members - 1)
    )
    slot = mm(slot, one_hot(image == iota((images, dp_count * rows), 0)))[0:1]
    row, column = iota((rows, dp_count * rows), 0), iota((rows, dp_count * rows), 1)
    pick = (slot == (row >> shift_of(tokens)).astype(F32)) & ((row & (tokens - 1)) == (column & (tokens - 1)))
    normed_ref[...] = mm(one_hot(pick), normed[...]).astype(BF16)
    for copy in copies:
        copy.wait()


def swaps(size, k):
    return [(i, i ^ k) for i in range(size)]


def on_device(
    query_rows,
    key_rows,
    value_rows,
    residual,
    out_proj,
    merge_gain,
    merger_proj,
    model_gain,
    image_grid,
    image_group,
    rollout_image,
    cotangent,
):
    dp_count, mp_count, rep_count = (lax.axis_size(a) for a in ("dp", "mp", "rep"))
    members = mp_count * rep_count
    patches, width = query_rows.shape
    tokens = patches // MERGE
    rows = members * tokens
    columns = merger_proj.shape[1]
    share = MERGE * width // dp_count
    devices = dp_count * members
    vmem, hbm = (pl.BlockSpec(memory_space=m) for m in (pltpu.VMEM, pltpu.HBM))
    scratch, dma = pltpu.VMEM, pltpu.SemaphoreType.DMA
    params = pltpu.CompilerParams(vmem_limit_bytes=VMEM_BYTES)
    stay = lambda *arrays: [pltpu.with_memory_space_constraint(x, pltpu.HBM) for x in arrays]
    grid = image_grid.T
    own_image = lambda: lax.axis_index(("dp", "mp", "rep"))
    dp_index = lambda: lax.axis_index("dp")
    indices = lambda: (lax.axis_index("dp"), lax.axis_index("mp"), lax.axis_index("rep"))
    shape = jax.ShapeDtypeStruct

    merged = pl.pallas_call(
        functools.partial(attention_kernel, own_image),
        out_shape=shape((patches, width), BF16),
        in_specs=[hbm] * 7,
        out_specs=vmem,
        scratch_shapes=[scratch(grid.shape, I32)]
        + [scratch((patches, width), BF16)] * 4
        + [scratch((width, width), BF16), scratch((width,), F32), dma((7,))],
        compiler_params=params,
        name="attention",
    )(*stay(grid, query_rows, key_rows, value_rows, residual, out_proj, merge_gain))

    images = image_group.shape[0]
    half_weight = (merger_proj.shape[0] // 2, columns)
    sums, place, weight_a = pl.pallas_call(
        functools.partial(cotangent_kernel, dp_index, members),
        out_shape=[shape((rows, columns), BF16), shape((1, images), I32), pltpu.VMEM(half_weight, BF16)],
        in_specs=[hbm] * 5,
        out_specs=[vmem] * 3,
        scratch_shapes=[
            scratch(rollout_image.shape, I32),
            scratch(grid.shape, I32),
            scratch((images,), I32),
            scratch(cotangent.shape, BF16),
            dma((5,)),
        ],
        compiler_params=params,
        name="cotangent_sums",
    )(*stay(rollout_image, grid, image_group, cotangent, merger_proj))

    pair = jnp.concatenate(
        [merged] + [lax.ppermute(merged, "rep", swaps(rep_count, a)) for a in range(1, rep_count)], axis=0
    )
    pieces = [pair] + [lax.ppermute(pair, "mp", swaps(mp_count, b)) for b in range(1, mp_count)]
    cores = 2
    sums = [sums] + [lax.ppermute(sums, "dp", swaps(dp_count, k)) for k in range(cores, dp_count, cores)]

    weight_b, gain, first_half = pl.pallas_call(
        prefetch_kernel,
        out_shape=[
            pltpu.VMEM(half_weight, BF16),
            pltpu.VMEM(model_gain.shape, F32),
            shape((len(sums) * rows, columns), BF16),
        ],
        in_specs=[pl.BlockSpec(memory_space=pl.ANY)] + [hbm] * 2 + [vmem] * len(sums),
        out_specs=[vmem] * 3,
        scratch_shapes=[dma((2,))],
        compiler_params=params,
        cost_estimate=pl.CostEstimate(flops=0, bytes_accessed=merger_proj.size, transcendentals=0),
        name="prefetch",
    )(pair, *stay(merger_proj, model_gain), *sums)
    second_half = lax.ppermute(first_half, "dp", swaps(dp_count, 1))

    *messages, partial = pl.pallas_call(
        functools.partial(projection_kernel, indices, dp_count, mp_count, rep_count),
        out_shape=[shape((rows, columns + share), BF16)] * dp_count + [shape((devices, 2, rows), F32)],
        in_specs=[vmem] * (mp_count + 6),
        out_specs=[vmem] * (dp_count + 1),
        scratch_shapes=[
            scratch((members * patches, width), BF16),
            scratch((members * patches, width), BF16),
            scratch((dp_count * rows, columns), BF16),
        ],
        compiler_params=params,
        name="projection",
    )(*pieces, first_half, second_half, weight_a, weight_b, gain, place)

    messages = [messages[0]] + [
        lax.ppermute(messages[k], "dp", swaps(dp_count, k)) for k in range(1, dp_count)
    ]
    partial = lax.all_to_all(partial, ("dp", "mp", "rep"), split_axis=0, concat_axis=0, tiled=True)

    normed_tokens, merger_grad = pl.pallas_call(
        functools.partial(final_kernel, dp_index, dp_count, float(columns * members)),
        out_shape=[shape((rows, columns), BF16), shape((share, columns), F32)],
        in_specs=[vmem] * (dp_count + 5),
        out_specs=[vmem, hbm],
        scratch_shapes=[
            scratch((dp_count * rows, columns), BF16),
            scratch((dp_count * rows, columns), BF16),
            scratch((dp_count * rows, share), BF16),
            scratch((share, columns), F32),
            scratch((dp_count * rows, columns), BF16),
            dma((-(-share // 256),)),
        ],
        compiler_params=params,
        name="final",
    )(*messages, partial, gain, place, first_half, second_half)
    return normed_tokens, merger_grad


def solution(mesh):
    return jax.shard_map(
        on_device,
        mesh=mesh,
        in_specs=(
            P(("dp", "mp", "rep"), None),
            P(("dp", "mp", "rep"), None),
            P(("dp", "mp", "rep"), None),
            P(("dp", "mp", "rep"), None),
            P(),
            P(),
            P(None, ("mp", "rep")),
            P(("mp", "rep")),
            P(),
            P(),
            P("dp"),
            P("dp", ("mp", "rep")),
        ),
        out_specs=(P("dp", ("mp", "rep")), P("dp", ("mp", "rep"))),
        check_vma=False,
    )
```

```python
import functools

import jax
import jax.numpy as jnp
from jax import lax
from jax.experimental import pallas as pl
from jax.experimental.pallas import tpu as pltpu
from jax.sharding import PartitionSpec as P

HEADS = 16
MERGE = 4
EPSILON = 1e-06
VMEM_BYTES = 24 * 1024 * 1024

F32 = jnp.float32
BF16 = jnp.bfloat16
I32 = jnp.int32


def iota(shape, dim):
    return lax.broadcasted_iota(I32, shape, dim)


def mm(a, b):
    return jnp.dot(a, b, preferred_element_type=F32)


def one_hot(condition):
    return jnp.where(condition, 1.0, 0.0).astype(BF16)


def shift_of(size):
    assert size & (size - 1) == 0
    return size.bit_length() - 1


def attention_kernel(
    own_image, grid_hbm, q_hbm, k_hbm, v_hbm, res_hbm, out_proj_hbm, gain_hbm, out_ref,
    grid_ref, q_ref, k_ref, v_ref, res_ref, proj, gain_ref, sems,
):
    pairs = [
        (q_hbm, q_ref), (k_hbm, k_ref), (grid_hbm, grid_ref), (v_hbm, v_ref),
        (out_proj_hbm, proj), (res_hbm, res_ref), (gain_hbm, gain_ref),
    ]
    loads = start_all(pairs, sems)
    rows, width = q_ref.shape
    head = width // HEADS
    image = own_image()
    feature = iota((1, width), 1)
    in_head = [(feature >= h * head) & (feature < (h + 1) * head) for h in range(HEADS)]
    loads[0].wait()
    q = q_ref[...].astype(F32)
    q_heads = jnp.concatenate([jnp.where(m, q, 0.0) for m in in_head], axis=0).astype(BF16)
    loads[1].wait()
    scores = lax.dot_general(
        q_heads, k_ref[...], (((1,), (1,)), ((), ())), preferred_element_type=F32
    ) * head ** (-0.5)
    loads[2].wait()
    counts = grid_ref[0:1, :] * grid_ref[1:2, :]
    valid = MERGE * jnp.sum(jnp.where(iota(counts.shape, 1) == image, counts, 0), axis=1, keepdims=True)
    scores = jnp.where(iota(scores.shape, 1) < valid, scores, -1e30)
    scores = jnp.exp(scores - jnp.max(scores, axis=1, keepdims=True))
    weights = (scores / jnp.sum(scores, axis=1, keepdims=True)).astype(BF16)
    loads[3].wait()
    spread = mm(weights, v_ref[...])
    attended = jnp.zeros((rows, width), F32)
    for h, m in enumerate(in_head):
        attended = attended + jnp.where(m, spread[h * rows : (h + 1) * rows], 0.0)
    loads[4].wait()
    mixed = mm(attended.astype(BF16), proj[...])
    loads[5].wait()
    mixed = res_ref[...].astype(F32) + mixed
    scale = lax.rsqrt(jnp.mean(mixed * mixed, axis=1, keepdims=True) + EPSILON)
    row_valid = jnp.where(iota((rows, 1), 0) < valid, 1.0, 0.0)
    loads[6].wait()
    out_ref[...] = (mixed * scale * gain_ref[...][None, :] * row_valid).astype(BF16)


def start_all(pairs, sems):
    loads = [pltpu.make_async_copy(source, to, sems.at[i]) for i, (source, to) in enumerate(pairs)]
    for load in loads:
        load.start()
    return loads


def cotangent_kernel(dp_index, members, roll_hbm, grid_hbm, group_hbm, cot_hbm, *refs):
    out_ref, place_ref, roll_ref, grid_ref, group_ref, cot_ref, sems = refs
    loads = start_all(
        [
            (group_hbm, group_ref), (roll_hbm, roll_ref), (grid_hbm, grid_ref), (cot_hbm, cot_ref),
        ],
        sems,
    )
    me = dp_index()
    rollouts = roll_ref.shape[0]
    slots = cot_ref.shape[0] // rollouts
    bits = shift_of(slots)
    wide = rollouts * slots
    rows = members * slots
    spread = one_hot((iota((rollouts, wide), 1) >> bits) == iota((rollouts, wide), 0))
    loads[0].wait()
    group = group_ref[...][None, :]
    images = group.shape[1]
    square = (images, images)
    column = jnp.sum(jnp.where(iota(square, 0) == iota(square, 1), group, 0), axis=1, keepdims=True)
    earlier = (column == group) & (iota(square, 0) < iota(square, 1))
    place = group * members + jnp.sum(jnp.where(earlier, 1, 0), axis=0, keepdims=True)
    place_ref[...] = place
    own_row = iota((rows, 1), 0)
    ours = place == me * members + (own_row >> bits)
    image = jnp.sum(jnp.where(ours, iota((rows, images), 1), 0), axis=1, keepdims=True)
    loads[1].wait()
    roll = roll_ref[...][None, :]
    high, low = (roll >> 8).astype(F32), (roll & 255).astype(F32)
    pair = jnp.concatenate([high, low] + [jnp.zeros((6, rollouts), F32)], axis=0).astype(BF16)
    pair = mm(pair, spread)
    roll_wide = (pair[0:1] * 256.0 + pair[1:2]).astype(I32)
    loads[2].wait()
    count = jnp.sum(jnp.where(ours, grid_ref[0:1, :] * grid_ref[1:2, :], 0), axis=1, keepdims=True)
    slot = own_row & (slots - 1)
    pick = (roll_wide == image) & (slot == (iota((1, wide), 1) & (slots - 1))) & (slot < count)
    loads[3].wait()
    out_ref[...] = mm(one_hot(pick), cot_ref[...]).astype(BF16)


def prefetch_kernel(after_ref, weight_hbm, gain_hbm, weight_ref, gain_ref, sems):
    del after_ref
    for load in start_all([(weight_hbm, weight_ref), (gain_hbm, gain_ref)], sems):
        load.wait()


def collect_sums(me, blocks, everything):
    rows = blocks[0].shape[0]
    for k, block in enumerate(blocks):
        everything[pl.ds(pl.multiple_of((me ^ k) * rows, rows), rows), :] = block[...]


def pick_sums(place, image, tokens, everything):
    rows, images = image.shape[0], place.shape[1]
    bits = shift_of(tokens)
    own = jnp.sum(jnp.where(iota((rows, images), 1) == image, place, 0), axis=1, keepdims=True)
    column = iota((1, everything.shape[0]), 1)
    pick = (own == (column >> bits)) & ((iota((rows, 1), 0) & (tokens - 1)) == (column & (tokens - 1)))
    return mm(one_hot(pick), everything[...])


def projection_kernel(indices, dp_count, mp_count, rep_count, *refs):
    pieces = refs[:mp_count]
    blocks = refs[mp_count : mp_count + dp_count]
    weight, gain_ref, place_ref = refs[mp_count + dp_count : mp_count + dp_count + 3]
    outs = refs[mp_count + dp_count + 3 :]
    messages, partial_ref = outs[:dp_count], outs[dp_count]
    gathered, merged, sums = outs[dp_count + 1 :]
    dp, mp, rep = indices()
    patches = pieces[0].shape[0] // rep_count
    tokens = patches // MERGE
    width = pieces[0].shape[1]
    members = mp_count * rep_count
    for b, piece in enumerate(pieces):
        for a in range(rep_count):
            place = (mp ^ b) * rep_count + (rep ^ a)
            gathered[pl.ds(pl.multiple_of(place * patches, patches), patches), :] = piece[
                a * patches : (a + 1) * patches, :
            ]
    rows = members * tokens
    everything = members * patches
    to, source = iota((everything, everything), 0), iota((everything, everything), 1)
    within = to & (rows - 1)
    wanted = (
        ((within >> shift_of(tokens)) << shift_of(patches))
        + ((within & (tokens - 1)) << shift_of(MERGE))
        + (to >> shift_of(rows))
    )
    merged[...] = mm(one_hot(wanted == source), gathered[...]).astype(BF16)
    columns = weight.shape[1]
    total = jnp.zeros((rows, columns), F32)
    for j in range(MERGE):
        total = total + mm(merged[j * rows : (j + 1) * rows, :], weight[j * width : (j + 1) * width, :])
    hidden = total.astype(BF16)
    collect_sums(dp, blocks, sums)
    image = dp * members + (iota((rows, 1), 0) >> shift_of(tokens))
    summed = pick_sums(place_ref[...], image, tokens, sums)
    wide = hidden.astype(F32)
    squares = jnp.sum(wide * wide, axis=1, keepdims=True)
    inner = jnp.sum(summed * gain_ref[...][None, :] * wide, axis=1, keepdims=True)
    diagonal = iota((rows, rows), 0) == iota((rows, rows), 1)
    both = jnp.concatenate(
        [jnp.sum(jnp.where(diagonal, x, 0.0), axis=0, keepdims=True) for x in (squares, inner)], axis=0
    )
    partial_ref[...] = jnp.broadcast_to(both[None], partial_ref.shape)
    share = MERGE * width // dp_count
    per_patch = width // share
    for k, message in enumerate(messages):
        message[:, 0:columns] = hidden
        target = dp ^ k
        first = pl.multiple_of((target >> shift_of(per_patch)) * rows, rows)
        for q in range(per_patch):

            @pl.when((target & (per_patch - 1)) == q)
            def _():
                message[:, columns : columns + share] = merged[
                    pl.ds(first, rows), q * share : (q + 1) * share
                ]


def final_kernel(dp_index, dp_count, model_width, *refs):
    messages = refs[:dp_count]
    blocks = refs[dp_count : 2 * dp_count]
    partial_ref, gain_ref, place_ref = refs[2 * dp_count : 2 * dp_count + 3]
    normed_ref, grad_hbm, token_grad, merged, grad, sums, sems = refs[2 * dp_count + 3 :]
    me = dp_index()
    rows, columns = normed_ref.shape
    members = partial_ref.shape[0] // dp_count
    share = merged.shape[1]
    tokens = rows // members
    gain = gain_ref[...][None, :]
    place = place_ref[...]
    images = place.shape[1]
    collect_sums(me, blocks, sums)
    diagonal = iota((rows, rows), 0) == iota((rows, rows), 1)
    inverses, factors = [], []
    for k in range(dp_count):
        both = jnp.sum(partial_ref[pl.ds(pl.multiple_of((me ^ k) * members, members), members)], axis=0)
        inverse = lax.rsqrt(both[0:1] / model_width + EPSILON)
        inverses.append(inverse)
        factors.append(inverse * inverse * inverse / model_width * both[1:2])
    upright = lambda x: jnp.sum(jnp.where(diagonal, x, 0.0), axis=1, keepdims=True)
    step = min(dp_count, max(1, 256 // rows))
    for k in range(0, dp_count, step):
        span = step * rows
        row = iota((span, 1), 0)
        image = ((me ^ (k + (row >> shift_of(rows)))) << shift_of(members)) + (
            (row >> shift_of(tokens)) & (members - 1)
        )
        summed = pick_sums(place, image, tokens, sums)
        inverse, factor, hidden = (
            jnp.concatenate(x, axis=0)
            for x in (
                [upright(x) for x in inverses[k : k + step]],
                [upright(x) for x in factors[k : k + step]],
                [m[:, 0:columns] for m in messages[k : k + step]],
            )
        )
        token_grad[k * rows : k * rows + span, :] = (
            inverse * (gain * summed) - hidden.astype(F32) * factor
        ).astype(BF16)
    for k, message in enumerate(messages):
        merged[k * rows : (k + 1) * rows, :] = message[:, columns : columns + share]
    copies = []
    chunk = min(share, 128)
    for c, at in enumerate(range(0, share, chunk)):
        size = min(chunk, share - at)
        grad[at : at + size, :] = lax.dot_general(
            merged[:, at : at + size], token_grad[...], (((0,), (0,)), ((), ())), preferred_element_type=F32
        )
        copies.append(pltpu.make_async_copy(grad.at[pl.ds(at, size), :], grad_hbm.at[pl.ds(at, size), :], sems.at[c]))
        copies[-1].start()
    slot = jnp.broadcast_to(place - me * members, (8, images))
    slot = jnp.where((slot >= 0) & (slot < members), slot, -1).astype(F32).astype(BF16)
    column = iota((images, dp_count * rows), 1)
    image = ((me ^ (column >> shift_of(rows))) << shift_of(members)) + (
        (column >> shift_of(tokens)) & (members - 1)
    )
    slot = mm(slot, one_hot(image == iota((images, dp_count * rows), 0)))[0:1]
    row, column = iota((rows, dp_count * rows), 0), iota((rows, dp_count * rows), 1)
    pick = (slot == (row >> shift_of(tokens)).astype(F32)) & ((row & (tokens - 1)) == (column & (tokens - 1)))
    inverse = jnp.sum(jnp.where(pick, jnp.concatenate(inverses, axis=1), 0.0), axis=1, keepdims=True)
    pick = one_hot(pick)
    hidden = jnp.zeros((rows, columns), F32)
    for k, message in enumerate(messages):
        hidden = hidden + mm(pick[:, k * rows : (k + 1) * rows], message[:, 0:columns])
    normed_ref[...] = (hidden * inverse * gain).astype(BF16)
    for copy in copies:
        copy.wait()


def swaps(size, k):
    return [(i, i ^ k) for i in range(size)]


def on_device(
    query_rows,
    key_rows,
    value_rows,
    residual,
    out_proj,
    merge_gain,
    merger_proj,
    model_gain,
    image_grid,
    image_group,
    rollout_image,
    cotangent,
):
    dp_count, mp_count, rep_count = (lax.axis_size(a) for a in ("dp", "mp", "rep"))
    members = mp_count * rep_count
    patches, width = query_rows.shape
    tokens = patches // MERGE
    rows = members * tokens
    columns = merger_proj.shape[1]
    share = MERGE * width // dp_count
    devices = dp_count * members
    vmem, hbm = (pl.BlockSpec(memory_space=m) for m in (pltpu.VMEM, pltpu.HBM))
    scratch, dma = pltpu.VMEM, pltpu.SemaphoreType.DMA
    params = pltpu.CompilerParams(vmem_limit_bytes=VMEM_BYTES)
    stay = lambda *arrays: [pltpu.with_memory_space_constraint(x, pltpu.HBM) for x in arrays]
    grid = image_grid.T
    own_image = lambda: lax.axis_index(("dp", "mp", "rep"))
    dp_index = lambda: lax.axis_index("dp")
    indices = lambda: (lax.axis_index("dp"), lax.axis_index("mp"), lax.axis_index("rep"))
    shape = jax.ShapeDtypeStruct

    merged = pl.pallas_call(
        functools.partial(attention_kernel, own_image),
        out_shape=shape((patches, width), BF16),
        in_specs=[hbm] * 7,
        out_specs=vmem,
        scratch_shapes=[scratch(grid.shape, I32)]
        + [scratch((patches, width), BF16)] * 4
        + [scratch((width, width), BF16), scratch((width,), F32), dma((7,))],
        compiler_params=params,
        name="attention",
    )(*stay(grid, query_rows, key_rows, value_rows, residual, out_proj, merge_gain))

    images = image_group.shape[0]
    sums, place = pl.pallas_call(
        functools.partial(cotangent_kernel, dp_index, members),
        out_shape=[shape((rows, columns), BF16), shape((1, images), I32)],
        in_specs=[hbm] * 4,
        out_specs=[vmem] * 2,
        scratch_shapes=[
            scratch(rollout_image.shape, I32),
            scratch(grid.shape, I32),
            scratch((images,), I32),
            scratch(cotangent.shape, BF16),
            dma((4,)),
        ],
        compiler_params=params,
        name="cotangent_sums",
    )(*stay(rollout_image, grid, image_group, cotangent))

    pair = jnp.concatenate(
        [merged] + [lax.ppermute(merged, "rep", swaps(rep_count, a)) for a in range(1, rep_count)], axis=0
    )
    pieces = [pair] + [lax.ppermute(pair, "mp", swaps(mp_count, b)) for b in range(1, mp_count)]
    blocks = [sums] + [lax.ppermute(sums, "dp", swaps(dp_count, k)) for k in range(1, dp_count)]

    weight, gain = pl.pallas_call(
        prefetch_kernel,
        out_shape=[pltpu.VMEM(merger_proj.shape, BF16), pltpu.VMEM(model_gain.shape, F32)],
        in_specs=[pl.BlockSpec(memory_space=pl.ANY)] + [hbm] * 2,
        out_specs=[vmem] * 2,
        scratch_shapes=[dma((2,))],
        compiler_params=params,
        cost_estimate=pl.CostEstimate(flops=0, bytes_accessed=2 * merger_proj.size, transcendentals=0),
        name="prefetch",
    )(pair, *stay(merger_proj, model_gain))

    *messages, partial = pl.pallas_call(
        functools.partial(projection_kernel, indices, dp_count, mp_count, rep_count),
        out_shape=[shape((rows, columns + share), BF16)] * dp_count + [shape((devices, 2, rows), F32)],
        in_specs=[vmem] * (mp_count + dp_count + 3),
        out_specs=[vmem] * (dp_count + 1),
        scratch_shapes=[
            scratch((members * patches, width), BF16),
            scratch((members * patches, width), BF16),
            scratch((dp_count * rows, columns), BF16),
        ],
        compiler_params=params,
        name="projection",
    )(*pieces, *blocks, weight, gain, place)

    messages = [messages[0]] + [
        lax.ppermute(messages[k], "dp", swaps(dp_count, k)) for k in range(1, dp_count)
    ]
    partial = lax.all_to_all(partial, ("dp", "mp", "rep"), split_axis=0, concat_axis=0, tiled=True)

    normed_tokens, merger_grad = pl.pallas_call(
        functools.partial(final_kernel, dp_index, dp_count, float(columns * members)),
        out_shape=[shape((rows, columns), BF16), shape((share, columns), F32)],
        in_specs=[vmem] * (2 * dp_count + 3),
        out_specs=[vmem, hbm],
        scratch_shapes=[
            scratch((dp_count * rows, columns), BF16),
            scratch((dp_count * rows, share), BF16),
            scratch((share, columns), F32),
            scratch((dp_count * rows, columns), BF16),
            dma((-(-share // 128),)),
        ],
        compiler_params=params,
        name="final",
    )(*messages, *blocks, partial, gain, place)
    return normed_tokens, merger_grad


def solution(mesh):
    return jax.shard_map(
        on_device,
        mesh=mesh,
        in_specs=(
            P(("dp", "mp", "rep"), None),
            P(("dp", "mp", "rep"), None),
            P(("dp", "mp", "rep"), None),
            P(("dp", "mp", "rep"), None),
            P(),
            P(),
            P(None, ("mp", "rep")),
            P(("mp", "rep")),
            P(),
            P(),
            P("dp"),
            P("dp", ("mp", "rep")),
        ),
        out_specs=(P("dp", ("mp", "rep")), P("dp", ("mp", "rep"))),
        check_vma=False,
    )
```

```python
import functools

import jax
import jax.numpy as jnp
from jax import lax
from jax.experimental import pallas as pl
from jax.experimental.pallas import tpu as pltpu
from jax.sharding import PartitionSpec as P

HEADS = 16
MERGE = 4
EPSILON = 1e-06
VMEM_BYTES = 24 * 1024 * 1024

F32 = jnp.float32
BF16 = jnp.bfloat16
I32 = jnp.int32


def iota(shape, dim):
    return lax.broadcasted_iota(I32, shape, dim)


def mm(a, b):
    return jnp.dot(a, b, preferred_element_type=F32)


def one_hot(condition):
    return jnp.where(condition, 1.0, 0.0).astype(BF16)


def shift_of(size):
    assert size & (size - 1) == 0
    return size.bit_length() - 1


def attention_kernel(
    own_image, grid_hbm, q_hbm, k_hbm, v_hbm, res_hbm, out_proj_hbm, gain_hbm, out_ref,
    grid_ref, q_ref, k_ref, v_ref, res_ref, proj, gain_ref, sems,
):
    rows, width = q_ref.shape
    head = width // HEADS
    parts = width // 256
    pairs = [(q_hbm, q_ref), (k_hbm, k_ref), (grid_hbm, grid_ref), (v_hbm, v_ref), (res_hbm, res_ref), (gain_hbm, gain_ref)]
    at = [pl.ds(c * 256, 256) for c in range(parts)]
    loads = start_all(pairs + [(out_proj_hbm.at[part, :], proj.at[part, :]) for part in at], sems)
    image = own_image()
    tiles = []
    for low in range(0, width, 128):
        first, last = low // head, (low + 127) // head
        feature = low + iota((1, 128), 1)
        inside = [(feature >= h * head) & (feature < (h + 1) * head) for h in range(first, last + 1)]
        tiles.append((slice(low, low + 128), first, last + 1, inside))
    loads[0].wait()
    loads[1].wait()
    scores = [0.0] * HEADS
    for lanes, first, last, inside in tiles:
        q = q_ref[:, lanes]
        q = jnp.concatenate([q * one_hot(m) for m in inside], axis=0)
        part = lax.dot_general(q, k_ref[:, lanes], (((1,), (1,)), ((), ())), preferred_element_type=F32)
        for i in range(last - first):
            scores[first + i] = scores[first + i] + part[i * rows : (i + 1) * rows]
    scores = jnp.concatenate(scores, axis=0) * head ** (-0.5)
    loads[2].wait()
    counts = grid_ref[0:1, :] * grid_ref[1:2, :]
    valid = MERGE * jnp.sum(jnp.where(iota(counts.shape, 1) == image, counts, 0), axis=1, keepdims=True)
    scores = jnp.where(iota(scores.shape, 1) < valid, scores, -1e30)
    scores = jnp.exp(scores - jnp.max(scores, axis=1, keepdims=True))
    weights = (scores / jnp.sum(scores, axis=1, keepdims=True)).astype(BF16)
    loads[3].wait()
    attended = []
    for lanes, first, last, inside in tiles:
        spread = mm(weights[first * rows : last * rows], v_ref[:, lanes])
        tile = spread[:rows]
        for i in range(1, last - first):
            tile = jnp.where(inside[i], spread[i * rows : (i + 1) * rows], tile)
        attended.append(tile.astype(BF16))
    loads[4].wait()
    mixed = res_ref[...].astype(F32)
    for c in range(parts):
        loads[6 + c].wait()
        mixed = mixed + mm(jnp.concatenate(attended[2 * c : 2 * c + 2], axis=1), proj[c * 256 : (c + 1) * 256, :])
    scale = lax.rsqrt(jnp.mean(mixed * mixed, axis=1, keepdims=True) + EPSILON)
    row_valid = jnp.where(iota((rows, 1), 0) < valid, 1.0, 0.0)
    loads[5].wait()
    out_ref[...] = (mixed * scale * gain_ref[...][None, :] * row_valid).astype(BF16)


def start_all(pairs, sems):
    loads = [pltpu.make_async_copy(source, to, sems.at[i]) for i, (source, to) in enumerate(pairs)]
    for load in loads:
        load.start()
    return loads


def cotangent_kernel(dp_index, members, roll_hbm, grid_hbm, group_hbm, cot_hbm, *refs):
    out_ref, place_ref, roll_ref, grid_ref, group_ref, cot_ref, sems = refs
    loads = start_all(
        [
            (group_hbm, group_ref), (roll_hbm, roll_ref), (grid_hbm, grid_ref), (cot_hbm, cot_ref),
        ],
        sems,
    )
    me = dp_index()
    rollouts = roll_ref.shape[0]
    slots = cot_ref.shape[0] // rollouts
    bits = shift_of(slots)
    wide = rollouts * slots
    rows = members * slots
    spread = one_hot((iota((rollouts, wide), 1) >> bits) == iota((rollouts, wide), 0))
    loads[0].wait()
    group = group_ref[...][None, :]
    images = group.shape[1]
    square = (images, images)
    column = jnp.sum(jnp.where(iota(square, 0) == iota(square, 1), group, 0), axis=1, keepdims=True)
    earlier = (column == group) & (iota(square, 0) < iota(square, 1))
    place = group * members + jnp.sum(jnp.where(earlier, 1, 0), axis=0, keepdims=True)
    place_ref[...] = place
    own_row = iota((rows, 1), 0)
    ours = place == me * members + (own_row >> bits)
    image = jnp.sum(jnp.where(ours, iota((rows, images), 1), 0), axis=1, keepdims=True)
    loads[1].wait()
    roll = roll_ref[...][None, :]
    high, low = (roll >> 8).astype(F32), (roll & 255).astype(F32)
    pair = jnp.concatenate([high, low] + [jnp.zeros((6, rollouts), F32)], axis=0).astype(BF16)
    pair = mm(pair, spread)
    roll_wide = (pair[0:1] * 256.0 + pair[1:2]).astype(I32)
    loads[2].wait()
    count = jnp.sum(jnp.where(ours, grid_ref[0:1, :] * grid_ref[1:2, :], 0), axis=1, keepdims=True)
    slot = own_row & (slots - 1)
    pick = (roll_wide == image) & (slot == (iota((1, wide), 1) & (slots - 1))) & (slot < count)
    loads[3].wait()
    out_ref[...] = mm(one_hot(pick), cot_ref[...]).astype(BF16)


def prefetch_kernel(after_ref, weight_hbm, gain_hbm, weight_ref, gain_ref, sems):
    del after_ref
    first = weight_hbm.at[pl.ds(0, weight_ref.shape[0]), :]
    for load in start_all([(first, weight_ref), (gain_hbm, gain_ref)], sems):
        load.wait()


def collect_sums(me, blocks, everything):
    rows = blocks[0].shape[0]
    for k, block in enumerate(blocks):
        everything[pl.ds(pl.multiple_of((me ^ k) * rows, rows), rows), :] = block[...]


def pick_sums(place, image, tokens, everything):
    rows, images = image.shape[0], place.shape[1]
    bits = shift_of(tokens)
    own = jnp.sum(jnp.where(iota((rows, images), 1) == image, place, 0), axis=1, keepdims=True)
    column = iota((1, everything.shape[0]), 1)
    pick = (own == (column >> bits)) & ((iota((rows, 1), 0) & (tokens - 1)) == (column & (tokens - 1)))
    return mm(one_hot(pick), everything[...])


def projection_kernel(indices, dp_count, mp_count, rep_count, *refs):
    pieces = refs[:mp_count]
    blocks = refs[mp_count : mp_count + dp_count]
    weight_hbm, weight, gain_ref, place_ref = refs[mp_count + dp_count : mp_count + dp_count + 4]
    outs = refs[mp_count + dp_count + 4 :]
    messages, partial_ref = outs[:dp_count], outs[dp_count]
    gathered, merged, sums, late_weight, sem = outs[dp_count + 1 :]
    ready, late = weight.shape[0], late_weight.shape[0]
    load = pltpu.make_async_copy(weight_hbm.at[pl.ds(ready, late), :], late_weight, sem)
    load.start()
    dp, mp, rep = indices()
    patches = pieces[0].shape[0] // rep_count
    tokens = patches // MERGE
    width = pieces[0].shape[1]
    members = mp_count * rep_count
    for b, piece in enumerate(pieces):
        for a in range(rep_count):
            place = (mp ^ b) * rep_count + (rep ^ a)
            gathered[pl.ds(pl.multiple_of(place * patches, patches), patches), :] = piece[
                a * patches : (a + 1) * patches, :
            ]
    rows = members * tokens
    everything = members * patches
    to, source = iota((everything, everything), 0), iota((everything, everything), 1)
    within = to & (rows - 1)
    wanted = (
        ((within >> shift_of(tokens)) << shift_of(patches))
        + ((within & (tokens - 1)) << shift_of(MERGE))
        + (to >> shift_of(rows))
    )
    merged[...] = mm(one_hot(wanted == source), gathered[...]).astype(BF16)
    columns = weight.shape[1]
    total = jnp.zeros((rows, columns), F32)
    for j in range(MERGE):
        left, first, last = merged[j * rows : (j + 1) * rows, :], j * width, (j + 1) * width
        middle = min(max(ready, first), last)
        if middle > first:
            total = total + mm(left[:, : middle - first], weight[first:middle, :])
        if middle < last:
            if middle == max(ready, first) and ready >= first:
                load.wait()
            total = total + mm(left[:, middle - first :], late_weight[middle - ready : last - ready, :])
    hidden = total.astype(BF16)
    collect_sums(dp, blocks, sums)
    image = dp * members + (iota((rows, 1), 0) >> shift_of(tokens))
    summed = pick_sums(place_ref[...], image, tokens, sums)
    wide = hidden.astype(F32)
    squares = jnp.sum(wide * wide, axis=1, keepdims=True)
    inner = jnp.sum(summed * gain_ref[...][None, :] * wide, axis=1, keepdims=True)
    diagonal = iota((rows, rows), 0) == iota((rows, rows), 1)
    both = jnp.concatenate(
        [jnp.sum(jnp.where(diagonal, x, 0.0), axis=0, keepdims=True) for x in (squares, inner)], axis=0
    )
    partial_ref[...] = jnp.broadcast_to(both[None], partial_ref.shape)
    share = MERGE * width // dp_count
    per_patch = width // share
    for k, message in enumerate(messages):
        message[:, 0:columns] = hidden
        target = dp ^ k
        first = pl.multiple_of((target >> shift_of(per_patch)) * rows, rows)
        for q in range(per_patch):

            @pl.when((target & (per_patch - 1)) == q)
            def _():
                message[:, columns : columns + share] = merged[
                    pl.ds(first, rows), q * share : (q + 1) * share
                ]


def final_kernel(dp_index, dp_count, model_width, *refs):
    messages = refs[:dp_count]
    blocks = refs[dp_count : 2 * dp_count]
    partial_ref, gain_ref, place_ref = refs[2 * dp_count : 2 * dp_count + 3]
    normed_ref, grad_hbm, token_grad, merged, grad, sums, sems = refs[2 * dp_count + 3 :]
    me = dp_index()
    rows, columns = normed_ref.shape
    members = partial_ref.shape[0] // dp_count
    share = merged.shape[1]
    tokens = rows // members
    gain = gain_ref[...][None, :]
    place = place_ref[...]
    images = place.shape[1]
    collect_sums(me, blocks, sums)
    diagonal = iota((rows, rows), 0) == iota((rows, rows), 1)
    inverses, factors = [], []
    for k in range(dp_count):
        both = jnp.sum(partial_ref[pl.ds(pl.multiple_of((me ^ k) * members, members), members)], axis=0)
        inverse = lax.rsqrt(both[0:1] / model_width + EPSILON)
        inverses.append(inverse)
        factors.append(inverse * inverse * inverse / model_width * both[1:2])
    upright = lambda x: jnp.sum(jnp.where(diagonal, x, 0.0), axis=1, keepdims=True)
    step = min(dp_count, max(1, 256 // rows))
    for k in range(0, dp_count, step):
        span = step * rows
        row = iota((span, 1), 0)
        image = ((me ^ (k + (row >> shift_of(rows)))) << shift_of(members)) + (
            (row >> shift_of(tokens)) & (members - 1)
        )
        summed = pick_sums(place, image, tokens, sums)
        inverse, factor, hidden = (
            jnp.concatenate(x, axis=0)
            for x in (
                [upright(x) for x in inverses[k : k + step]],
                [upright(x) for x in factors[k : k + step]],
                [m[:, 0:columns] for m in messages[k : k + step]],
            )
        )
        token_grad[k * rows : k * rows + span, :] = (
            inverse * (gain * summed) - hidden.astype(F32) * factor
        ).astype(BF16)
    for k, message in enumerate(messages):
        merged[k * rows : (k + 1) * rows, :] = message[:, columns : columns + share]
    copies = []
    chunk = min(share, 128)
    for c, at in enumerate(range(0, share, chunk)):
        size = min(chunk, share - at)
        grad[at : at + size, :] = lax.dot_general(
            merged[:, at : at + size], token_grad[...], (((0,), (0,)), ((), ())), preferred_element_type=F32
        )
        copies.append(pltpu.make_async_copy(grad.at[pl.ds(at, size), :], grad_hbm.at[pl.ds(at, size), :], sems.at[c]))
        copies[-1].start()
    slot = jnp.broadcast_to(place - me * members, (8, images))
    slot = jnp.where((slot >= 0) & (slot < members), slot, -1).astype(F32).astype(BF16)
    column = iota((images, dp_count * rows), 1)
    image = ((me ^ (column >> shift_of(rows))) << shift_of(members)) + (
        (column >> shift_of(tokens)) & (members - 1)
    )
    slot = mm(slot, one_hot(image == iota((images, dp_count * rows), 0)))[0:1]
    row, column = iota((rows, dp_count * rows), 0), iota((rows, dp_count * rows), 1)
    pick = (slot == (row >> shift_of(tokens)).astype(F32)) & ((row & (tokens - 1)) == (column & (tokens - 1)))
    inverse = jnp.sum(jnp.where(pick, jnp.concatenate(inverses, axis=1), 0.0), axis=1, keepdims=True)
    pick = one_hot(pick)
    hidden = jnp.zeros((rows, columns), F32)
    for k, message in enumerate(messages):
        hidden = hidden + mm(pick[:, k * rows : (k + 1) * rows], message[:, 0:columns])
    normed_ref[...] = (hidden * inverse * gain).astype(BF16)
    for copy in copies:
        copy.wait()


def swaps(size, k):
    return [(i, i ^ k) for i in range(size)]


def on_device(
    query_rows,
    key_rows,
    value_rows,
    residual,
    out_proj,
    merge_gain,
    merger_proj,
    model_gain,
    image_grid,
    image_group,
    rollout_image,
    cotangent,
):
    dp_count, mp_count, rep_count = (lax.axis_size(a) for a in ("dp", "mp", "rep"))
    members = mp_count * rep_count
    patches, width = query_rows.shape
    tokens = patches // MERGE
    rows = members * tokens
    columns = merger_proj.shape[1]
    share = MERGE * width // dp_count
    devices = dp_count * members
    vmem, hbm = (pl.BlockSpec(memory_space=m) for m in (pltpu.VMEM, pltpu.HBM))
    scratch, dma = pltpu.VMEM, pltpu.SemaphoreType.DMA
    params = pltpu.CompilerParams(vmem_limit_bytes=VMEM_BYTES)
    stay = lambda *arrays: [pltpu.with_memory_space_constraint(x, pltpu.HBM) for x in arrays]
    grid = image_grid.T
    own_image = lambda: lax.axis_index(("dp", "mp", "rep"))
    dp_index = lambda: lax.axis_index("dp")
    indices = lambda: (lax.axis_index("dp"), lax.axis_index("mp"), lax.axis_index("rep"))
    shape = jax.ShapeDtypeStruct

    merged = pl.pallas_call(
        functools.partial(attention_kernel, own_image),
        out_shape=shape((patches, width), BF16),
        in_specs=[hbm] * 7,
        out_specs=vmem,
        scratch_shapes=[scratch(grid.shape, I32)]
        + [scratch((patches, width), BF16)] * 4
        + [scratch((width, width), BF16), scratch((width,), F32), dma((6 + width // 256,))],
        compiler_params=params,
        name="attention",
    )(*stay(grid, query_rows, key_rows, value_rows, residual, out_proj, merge_gain))

    images = image_group.shape[0]
    sums, place = pl.pallas_call(
        functools.partial(cotangent_kernel, dp_index, members),
        out_shape=[shape((rows, columns), BF16), shape((1, images), I32)],
        in_specs=[hbm] * 4,
        out_specs=[vmem] * 2,
        scratch_shapes=[
            scratch(rollout_image.shape, I32),
            scratch(grid.shape, I32),
            scratch((images,), I32),
            scratch(cotangent.shape, BF16),
            dma((4,)),
        ],
        compiler_params=params,
        name="cotangent_sums",
    )(*stay(rollout_image, grid, image_group, cotangent))

    pair = jnp.concatenate(
        [merged] + [lax.ppermute(merged, "rep", swaps(rep_count, a)) for a in range(1, rep_count)], axis=0
    )
    pieces = [pair] + [lax.ppermute(pair, "mp", swaps(mp_count, b)) for b in range(1, mp_count)]
    blocks = {0: sums}
    for k in range(2, dp_count, 2):
        blocks[k] = lax.ppermute(sums, "dp", swaps(dp_count, k))
    for k in range(0, dp_count, 2):
        blocks[k + 1] = lax.ppermute(blocks[k], "dp", swaps(dp_count, 1))
    blocks = [blocks[k] for k in range(dp_count)]

    early = MERGE * width * 3 // 4
    weight, gain = pl.pallas_call(
        prefetch_kernel,
        out_shape=[pltpu.VMEM((early, columns), BF16), pltpu.VMEM(model_gain.shape, F32)],
        in_specs=[pl.BlockSpec(memory_space=pl.ANY)] + [hbm] * 2,
        out_specs=[vmem] * 2,
        scratch_shapes=[dma((2,))],
        compiler_params=params,
        cost_estimate=pl.CostEstimate(flops=0, bytes_accessed=2 * merger_proj.size, transcendentals=0),
        name="prefetch",
    )(pair, *stay(merger_proj, model_gain))

    *messages, partial = pl.pallas_call(
        functools.partial(projection_kernel, indices, dp_count, mp_count, rep_count),
        out_shape=[shape((rows, columns + share), BF16)] * dp_count + [shape((devices, 2, rows), F32)],
        in_specs=[vmem] * (mp_count + dp_count) + [hbm] + [vmem] * 3,
        out_specs=[vmem] * (dp_count + 1),
        scratch_shapes=[
            scratch((members * patches, width), BF16),
            scratch((members * patches, width), BF16),
            scratch((dp_count * rows, columns), BF16),
            scratch((MERGE * width - early, columns), BF16),
            dma,
        ],
        compiler_params=params,
        name="projection",
    )(*pieces, *blocks, *stay(merger_proj), weight, gain, place)

    messages = [messages[0]] + [
        lax.ppermute(messages[k], "dp", swaps(dp_count, k)) for k in range(1, dp_count)
    ]
    partial = lax.all_to_all(partial, ("dp", "mp", "rep"), split_axis=0, concat_axis=0, tiled=True)

    normed_tokens, merger_grad = pl.pallas_call(
        functools.partial(final_kernel, dp_index, dp_count, float(columns * members)),
        out_shape=[shape((rows, columns), BF16), shape((share, columns), F32)],
        in_specs=[vmem] * (2 * dp_count + 3),
        out_specs=[vmem, hbm],
        scratch_shapes=[
            scratch((dp_count * rows, columns), BF16),
            scratch((dp_count * rows, share), BF16),
            scratch((share, columns), F32),
            scratch((dp_count * rows, columns), BF16),
            dma((-(-share // 128),)),
        ],
        compiler_params=params,
        name="final",
    )(*messages, *blocks, partial, gain, place)
    return normed_tokens, merger_grad


def solution(mesh):
    return jax.shard_map(
        on_device,
        mesh=mesh,
        in_specs=(
            P(("dp", "mp", "rep"), None),
            P(("dp", "mp", "rep"), None),
            P(("dp", "mp", "rep"), None),
            P(("dp", "mp", "rep"), None),
            P(),
            P(),
            P(None, ("mp", "rep")),
            P(("mp", "rep")),
            P(),
            P(),
            P("dp"),
            P("dp", ("mp", "rep")),
        ),
        out_specs=(P("dp", ("mp", "rep")), P("dp", ("mp", "rep"))),
        check_vma=False,
    )
```

```python
import functools

import jax
import jax.numpy as jnp
from jax import lax
from jax.experimental import pallas as pl
from jax.experimental.pallas import tpu as pltpu
from jax.sharding import PartitionSpec as P

HEADS = 16
MERGE = 4
EPSILON = 1e-06
PARTS = (5, 12, 3)
VMEM_BYTES = 24 * 1024 * 1024

F32 = jnp.float32
BF16 = jnp.bfloat16
I32 = jnp.int32


def iota(shape, dim):
    return lax.broadcasted_iota(I32, shape, dim)


def mm(a, b):
    return jnp.dot(a, b, preferred_element_type=F32)


def one_hot(condition):
    return jnp.where(condition, 1.0, 0.0).astype(BF16)


def shift_of(size):
    assert size & (size - 1) == 0
    return size.bit_length() - 1


def attention_kernel(
    own_image, grid_hbm, q_hbm, k_hbm, v_hbm, res_hbm, out_proj_hbm, gain_hbm, out_ref,
    grid_ref, q_ref, k_ref, v_ref, res_ref, proj, gain_ref, sems,
):
    rows, width = q_ref.shape
    head = width // HEADS
    parts = width // 256
    pairs = [(q_hbm, q_ref), (k_hbm, k_ref), (grid_hbm, grid_ref), (v_hbm, v_ref), (res_hbm, res_ref), (gain_hbm, gain_ref)]
    at = [pl.ds(c * 256, 256) for c in range(parts)]
    loads = start_all(pairs + [(out_proj_hbm.at[part, :], proj.at[part, :]) for part in at], sems)
    image = own_image()
    tiles = []
    for low in range(0, width, 128):
        first, last = low // head, (low + 127) // head
        feature = low + iota((1, 128), 1)
        inside = [(feature >= h * head) & (feature < (h + 1) * head) for h in range(first, last + 1)]
        tiles.append((slice(low, low + 128), first, last + 1, inside))
    loads[0].wait()
    loads[1].wait()
    scores = [0.0] * HEADS
    for lanes, first, last, inside in tiles:
        q = q_ref[:, lanes]
        q = jnp.concatenate([q * one_hot(m) for m in inside], axis=0)
        part = lax.dot_general(q, k_ref[:, lanes], (((1,), (1,)), ((), ())), preferred_element_type=F32)
        for i in range(last - first):
            scores[first + i] = scores[first + i] + part[i * rows : (i + 1) * rows]
    scores = jnp.concatenate(scores, axis=0) * head ** (-0.5)
    loads[2].wait()
    counts = grid_ref[0:1, :] * grid_ref[1:2, :]
    valid = MERGE * jnp.sum(jnp.where(iota(counts.shape, 1) == image, counts, 0), axis=1, keepdims=True)
    scores = jnp.where(iota(scores.shape, 1) < valid, scores, -1e30)
    scores = jnp.exp(scores - jnp.max(scores, axis=1, keepdims=True))
    weights = (scores / jnp.sum(scores, axis=1, keepdims=True)).astype(BF16)
    loads[3].wait()
    attended = []
    for lanes, first, last, inside in tiles:
        spread = mm(weights[first * rows : last * rows], v_ref[:, lanes])
        tile = spread[:rows]
        for i in range(1, last - first):
            tile = jnp.where(inside[i], spread[i * rows : (i + 1) * rows], tile)
        attended.append(tile.astype(BF16))
    loads[4].wait()
    mixed = res_ref[...].astype(F32)
    for c in range(parts):
        loads[6 + c].wait()
        mixed = mixed + mm(jnp.concatenate(attended[2 * c : 2 * c + 2], axis=1), proj[c * 256 : (c + 1) * 256, :])
    scale = lax.rsqrt(jnp.mean(mixed * mixed, axis=1, keepdims=True) + EPSILON)
    row_valid = jnp.where(iota((rows, 1), 0) < valid, 1.0, 0.0)
    loads[5].wait()
    out_ref[...] = (mixed * scale * gain_ref[...][None, :] * row_valid).astype(BF16)


def start_all(pairs, sems):
    loads = [pltpu.make_async_copy(source, to, sems.at[i]) for i, (source, to) in enumerate(pairs)]
    for load in loads:
        load.start()
    return loads


def cotangent_kernel(dp_index, members, roll_hbm, grid_hbm, group_hbm, cot_hbm, weight_hbm, *refs):
    out_ref, place_ref, weight_ref, roll_ref, grid_ref, group_ref, cot_ref, sems = refs
    first = weight_hbm.at[pl.ds(0, weight_ref.shape[0]), :]
    loads = start_all(
        [
            (group_hbm, group_ref), (roll_hbm, roll_ref), (grid_hbm, grid_ref), (cot_hbm, cot_ref),
            (first, weight_ref),
        ],
        sems,
    )
    me = dp_index()
    rollouts = roll_ref.shape[0]
    slots = cot_ref.shape[0] // rollouts
    bits = shift_of(slots)
    wide = rollouts * slots
    rows = members * slots
    spread = one_hot((iota((rollouts, wide), 1) >> bits) == iota((rollouts, wide), 0))
    loads[0].wait()
    group = group_ref[...][None, :]
    images = group.shape[1]
    square = (images, images)
    column = jnp.sum(jnp.where(iota(square, 0) == iota(square, 1), group, 0), axis=1, keepdims=True)
    earlier = (column == group) & (iota(square, 0) < iota(square, 1))
    place = group * members + jnp.sum(jnp.where(earlier, 1, 0), axis=0, keepdims=True)
    place_ref[...] = place
    own_row = iota((rows, 1), 0)
    ours = place == me * members + (own_row >> bits)
    image = jnp.sum(jnp.where(ours, iota((rows, images), 1), 0), axis=1, keepdims=True)
    loads[1].wait()
    roll = roll_ref[...][None, :]
    high, low = (roll >> 8).astype(F32), (roll & 255).astype(F32)
    pair = jnp.concatenate([high, low] + [jnp.zeros((6, rollouts), F32)], axis=0).astype(BF16)
    pair = mm(pair, spread)
    roll_wide = (pair[0:1] * 256.0 + pair[1:2]).astype(I32)
    loads[2].wait()
    count = jnp.sum(jnp.where(ours, grid_ref[0:1, :] * grid_ref[1:2, :], 0), axis=1, keepdims=True)
    slot = own_row & (slots - 1)
    pick = (roll_wide == image) & (slot == (iota((1, wide), 1) & (slots - 1))) & (slot < count)
    loads[3].wait()
    out_ref[...] = mm(one_hot(pick), cot_ref[...]).astype(BF16)
    loads[4].wait()


def prefetch_kernel(start, after_ref, weight_hbm, gain_hbm, weight_ref, gain_ref, sems):
    del after_ref
    part = weight_hbm.at[pl.ds(start, weight_ref.shape[0]), :]
    for load in start_all([(part, weight_ref), (gain_hbm, gain_ref)], sems):
        load.wait()


def collect_sums(me, blocks, everything):
    rows = blocks[0].shape[0]
    for k, block in enumerate(blocks):
        everything[pl.ds(pl.multiple_of((me ^ k) * rows, rows), rows), :] = block[...]


def pick_sums(place, image, tokens, everything):
    rows, images = image.shape[0], place.shape[1]
    bits = shift_of(tokens)
    own = jnp.sum(jnp.where(iota((rows, images), 1) == image, place, 0), axis=1, keepdims=True)
    column = iota((1, everything.shape[0]), 1)
    pick = (own == (column >> bits)) & ((iota((rows, 1), 0) & (tokens - 1)) == (column & (tokens - 1)))
    return mm(one_hot(pick), everything[...])


def projection_kernel(indices, dp_count, mp_count, rep_count, *refs):
    pieces = refs[:mp_count]
    blocks = refs[mp_count : mp_count + dp_count]
    weight_hbm, *weights, gain_ref, place_ref = refs[mp_count + dp_count : mp_count + dp_count + 5]
    outs = refs[mp_count + dp_count + 5 :]
    messages, partial_ref, summed_ref = outs[:dp_count], outs[dp_count], outs[dp_count + 1]
    gathered, merged, sums, late_weight, sem = outs[dp_count + 2 :]
    late = late_weight.shape[0]
    load = pltpu.make_async_copy(weight_hbm.at[pl.ds(weight_hbm.shape[0] - late, late), :], late_weight, sem)
    load.start()
    dp, mp, rep = indices()
    patches = pieces[0].shape[0] // rep_count
    tokens = patches // MERGE
    width = pieces[0].shape[1]
    members = mp_count * rep_count
    for b, piece in enumerate(pieces):
        for a in range(rep_count):
            place = (mp ^ b) * rep_count + (rep ^ a)
            gathered[pl.ds(pl.multiple_of(place * patches, patches), patches), :] = piece[
                a * patches : (a + 1) * patches, :
            ]
    rows = members * tokens
    everything = members * patches
    to, source = iota((everything, everything), 0), iota((everything, everything), 1)
    within = to & (rows - 1)
    wanted = (
        ((within >> shift_of(tokens)) << shift_of(patches))
        + ((within & (tokens - 1)) << shift_of(MERGE))
        + (to >> shift_of(rows))
    )
    merged[...] = mm(one_hot(wanted == source), gathered[...]).astype(BF16)
    columns = weight_hbm.shape[1]
    total = jnp.zeros((rows, columns), F32)
    start = 0
    for weight in [*weights, late_weight]:
        if weight is late_weight:
            load.wait()
        end = start + weight.shape[0]
        for j in range(MERGE):
            low, high = max(start, j * width), min(end, (j + 1) * width)
            if low < high:
                left = merged[j * rows : (j + 1) * rows, low - j * width : high - j * width]
                total = total + mm(left, weight[low - start : high - start, :])
        start = end
    hidden = total.astype(BF16)
    collect_sums(dp, blocks, sums)
    step = min(dp_count, max(1, 256 // rows))
    row = iota((step * rows, 1), 0)
    for k in range(0, dp_count, step):
        image = ((dp ^ (k + (row >> shift_of(rows)))) << shift_of(members)) + (
            (row >> shift_of(tokens)) & (members - 1)
        )
        picked = pick_sums(place_ref[...], image, tokens, sums) * gain_ref[...][None, :]
        summed_ref[k * rows : (k + step) * rows, :] = picked
    summed = summed_ref[0:rows, :]
    wide = hidden.astype(F32)
    squares = jnp.sum(wide * wide, axis=1, keepdims=True)
    inner = jnp.sum(summed * wide, axis=1, keepdims=True)
    diagonal = iota((rows, rows), 0) == iota((rows, rows), 1)
    both = jnp.concatenate(
        [jnp.sum(jnp.where(diagonal, x, 0.0), axis=0, keepdims=True) for x in (squares, inner)], axis=0
    )
    partial_ref[...] = jnp.broadcast_to(both[None], partial_ref.shape)
    share = MERGE * width // dp_count
    per_patch = width // share
    for k, message in enumerate(messages):
        message[:, 0:columns] = hidden
        target = dp ^ k
        first = pl.multiple_of((target >> shift_of(per_patch)) * rows, rows)
        for q in range(per_patch):

            @pl.when((target & (per_patch - 1)) == q)
            def _():
                message[:, columns : columns + share] = merged[
                    pl.ds(first, rows), q * share : (q + 1) * share
                ]


def final_kernel(dp_index, dp_count, model_width, *refs):
    messages = refs[:dp_count]
    summed_ref, partial_ref, gain_ref, place_ref = refs[dp_count : dp_count + 4]
    normed_ref, grad_hbm, token_grad, grad, sems = refs[dp_count + 4 :]
    me = dp_index()
    rows, columns = normed_ref.shape
    members = partial_ref.shape[0] // dp_count
    share = grad.shape[0]
    tokens = rows // members
    gain = gain_ref[...][None, :]
    place = place_ref[...]
    images = place.shape[1]
    diagonal = iota((rows, rows), 0) == iota((rows, rows), 1)
    inverses, factors = [], []
    for k in range(dp_count):
        both = jnp.sum(partial_ref[pl.ds(pl.multiple_of((me ^ k) * members, members), members)], axis=0)
        inverse = lax.rsqrt(both[0:1] / model_width + EPSILON)
        inverses.append(inverse)
        factors.append(inverse * inverse * inverse / model_width * both[1:2])
    upright = lambda x: jnp.sum(jnp.where(diagonal, x, 0.0), axis=1, keepdims=True)
    step = min(dp_count, max(1, 256 // rows))
    for k in range(0, dp_count, step):
        span = step * rows
        inverse, factor, hidden = (
            jnp.concatenate(x, axis=0)
            for x in (
                [upright(x) for x in inverses[k : k + step]],
                [upright(x) for x in factors[k : k + step]],
                [m[:, 0:columns] for m in messages[k : k + step]],
            )
        )
        token_grad[k * rows : k * rows + span, :] = (
            inverse * summed_ref[k * rows : k * rows + span, :] - hidden.astype(F32) * factor
        ).astype(BF16)
    copies = []
    chunk = min(share, 128)
    for c, at in enumerate(range(0, share, chunk)):
        size = min(chunk, share - at)
        left = jnp.concatenate([m[:, columns + at : columns + at + size] for m in messages], axis=0)
        grad[at : at + size, :] = lax.dot_general(
            left, token_grad[...], (((0,), (0,)), ((), ())), preferred_element_type=F32
        )
        copies.append(pltpu.make_async_copy(grad.at[pl.ds(at, size), :], grad_hbm.at[pl.ds(at, size), :], sems.at[c]))
        copies[-1].start()
    slot = jnp.broadcast_to(place - me * members, (8, images))
    slot = jnp.where((slot >= 0) & (slot < members), slot, -1).astype(F32).astype(BF16)
    column = iota((images, dp_count * rows), 1)
    image = ((me ^ (column >> shift_of(rows))) << shift_of(members)) + (
        (column >> shift_of(tokens)) & (members - 1)
    )
    slot = mm(slot, one_hot(image == iota((images, dp_count * rows), 0)))[0:1]
    row, column = iota((rows, dp_count * rows), 0), iota((rows, dp_count * rows), 1)
    pick = (slot == (row >> shift_of(tokens)).astype(F32)) & ((row & (tokens - 1)) == (column & (tokens - 1)))
    inverse = jnp.sum(jnp.where(pick, jnp.concatenate(inverses, axis=1), 0.0), axis=1, keepdims=True)
    pick = one_hot(pick)
    hidden = jnp.zeros((rows, columns), F32)
    for k, message in enumerate(messages):
        hidden = hidden + mm(pick[:, k * rows : (k + 1) * rows], message[:, 0:columns])
    normed_ref[...] = (hidden * inverse * gain).astype(BF16)
    for copy in copies:
        copy.wait()


def swaps(size, k):
    return [(i, i ^ k) for i in range(size)]


def on_device(
    query_rows,
    key_rows,
    value_rows,
    residual,
    out_proj,
    merge_gain,
    merger_proj,
    model_gain,
    image_grid,
    image_group,
    rollout_image,
    cotangent,
):
    dp_count, mp_count, rep_count = (lax.axis_size(a) for a in ("dp", "mp", "rep"))
    members = mp_count * rep_count
    patches, width = query_rows.shape
    tokens = patches // MERGE
    rows = members * tokens
    columns = merger_proj.shape[1]
    share = MERGE * width // dp_count
    devices = dp_count * members
    vmem, hbm = (pl.BlockSpec(memory_space=m) for m in (pltpu.VMEM, pltpu.HBM))
    scratch, dma = pltpu.VMEM, pltpu.SemaphoreType.DMA
    params = pltpu.CompilerParams(vmem_limit_bytes=VMEM_BYTES)
    stay = lambda *arrays: [pltpu.with_memory_space_constraint(x, pltpu.HBM) for x in arrays]
    grid = image_grid.T
    own_image = lambda: lax.axis_index(("dp", "mp", "rep"))
    dp_index = lambda: lax.axis_index("dp")
    indices = lambda: (lax.axis_index("dp"), lax.axis_index("mp"), lax.axis_index("rep"))
    shape = jax.ShapeDtypeStruct

    merged = pl.pallas_call(
        functools.partial(attention_kernel, own_image),
        out_shape=shape((patches, width), BF16),
        in_specs=[hbm] * 7,
        out_specs=vmem,
        scratch_shapes=[scratch(grid.shape, I32)]
        + [scratch((patches, width), BF16)] * 4
        + [scratch((width, width), BF16), scratch((width,), F32), dma((6 + width // 256,))],
        compiler_params=params,
        name="attention",
    )(*stay(grid, query_rows, key_rows, value_rows, residual, out_proj, merge_gain))

    images = image_group.shape[0]
    parts = [MERGE * width * part // sum(PARTS) for part in PARTS]
    sums, place, weight_a = pl.pallas_call(
        functools.partial(cotangent_kernel, dp_index, members),
        out_shape=[
            shape((rows, columns), BF16), shape((1, images), I32), pltpu.VMEM((parts[0], columns), BF16)
        ],
        in_specs=[hbm] * 5,
        out_specs=[vmem] * 3,
        scratch_shapes=[
            scratch(rollout_image.shape, I32),
            scratch(grid.shape, I32),
            scratch((images,), I32),
            scratch(cotangent.shape, BF16),
            dma((5,)),
        ],
        compiler_params=params,
        name="cotangent_sums",
    )(*stay(rollout_image, grid, image_group, cotangent, merger_proj))

    pair = jnp.concatenate(
        [merged] + [lax.ppermute(merged, "rep", swaps(rep_count, a)) for a in range(1, rep_count)], axis=0
    )
    pieces = [pair] + [lax.ppermute(pair, "mp", swaps(mp_count, b)) for b in range(1, mp_count)]
    blocks = {0: sums}
    for k in range(2, dp_count, 2):
        blocks[k] = lax.ppermute(sums, "dp", swaps(dp_count, k))
    for k in range(0, dp_count, 2):
        blocks[k + 1] = lax.ppermute(blocks[k], "dp", swaps(dp_count, 1))
    blocks = [blocks[k] for k in range(dp_count)]

    weight_b, gain = pl.pallas_call(
        functools.partial(prefetch_kernel, parts[0]),
        out_shape=[pltpu.VMEM((parts[1], columns), BF16), pltpu.VMEM(model_gain.shape, F32)],
        in_specs=[pl.BlockSpec(memory_space=pl.ANY)] + [hbm] * 2,
        out_specs=[vmem] * 2,
        scratch_shapes=[dma((2,))],
        compiler_params=params,
        cost_estimate=pl.CostEstimate(flops=0, bytes_accessed=2 * merger_proj.size, transcendentals=0),
        name="prefetch",
    )(pair, *stay(merger_proj, model_gain))

    *messages, partial, summed = pl.pallas_call(
        functools.partial(projection_kernel, indices, dp_count, mp_count, rep_count),
        out_shape=[shape((rows, columns + share), BF16)] * dp_count + [shape((devices, 2, rows), F32), shape((dp_count * rows, columns), F32)],
        in_specs=[vmem] * (mp_count + dp_count) + [hbm] + [vmem] * 4,
        out_specs=[vmem] * (dp_count + 2),
        scratch_shapes=[
            scratch((members * patches, width), BF16),
            scratch((members * patches, width), BF16),
            scratch((dp_count * rows, columns), BF16),
            scratch((parts[2], columns), BF16),
            dma,
        ],
        compiler_params=params,
        name="projection",
    )(*pieces, *blocks, *stay(merger_proj), weight_a, weight_b, gain, place)

    messages = [messages[0]] + [
        lax.ppermute(messages[k], "dp", swaps(dp_count, k)) for k in range(1, dp_count)
    ]
    partial = lax.all_to_all(partial, ("dp", "mp", "rep"), split_axis=0, concat_axis=0, tiled=True)

    normed_tokens, merger_grad = pl.pallas_call(
        functools.partial(final_kernel, dp_index, dp_count, float(columns * members)),
        out_shape=[shape((rows, columns), BF16), shape((share, columns), F32)],
        in_specs=[vmem] * (dp_count + 4),
        out_specs=[vmem, hbm],
        scratch_shapes=[
            scratch((dp_count * rows, columns), BF16),
            scratch((share, columns), F32),
            dma((-(-share // 128),)),
        ],
        compiler_params=params,
        name="final",
    )(*messages, summed, partial, gain, place)
    return normed_tokens, merger_grad


def solution(mesh):
    return jax.shard_map(
        on_device,
        mesh=mesh,
        in_specs=(
            P(("dp", "mp", "rep"), None),
            P(("dp", "mp", "rep"), None),
            P(("dp", "mp", "rep"), None),
            P(("dp", "mp", "rep"), None),
            P(),
            P(),
            P(None, ("mp", "rep")),
            P(("mp", "rep")),
            P(),
            P(),
            P("dp"),
            P("dp", ("mp", "rep")),
        ),
        out_specs=(P("dp", ("mp", "rep")), P("dp", ("mp", "rep"))),
        check_vma=False,
    )
```

```python
import functools

import jax
import jax.numpy as jnp
from jax import lax
from jax.experimental import pallas as pl
from jax.experimental.pallas import tpu as pltpu
from jax.sharding import PartitionSpec as P

HEADS = 16
MERGE = 4
EPSILON = 1e-06
PARTS = (14, 6)
VMEM_BYTES = 24 * 1024 * 1024

F32 = jnp.float32
BF16 = jnp.bfloat16
I32 = jnp.int32


def iota(shape, dim):
    return lax.broadcasted_iota(I32, shape, dim)


def mm(a, b):
    return jnp.dot(a, b, preferred_element_type=F32)


def one_hot(condition):
    return jnp.where(condition, 1.0, 0.0).astype(BF16)


def shift_of(size):
    assert size & (size - 1) == 0
    return size.bit_length() - 1


def attention_kernel(
    indices, members,
    grid_hbm, q_hbm, k_hbm, v_hbm, res_hbm, out_proj_hbm, gain_hbm, roll_hbm, group_hbm, cot_hbm,
    out_ref, sums_ref, place_ref,
    grid_ref, q_ref, k_ref, v_ref, res_ref, proj, gain_ref, roll_ref, group_ref, cot_ref, sems,
):
    rows, width = q_ref.shape
    head = width // HEADS
    parts = width // 256
    pairs = [(q_hbm, q_ref), (k_hbm, k_ref), (grid_hbm, grid_ref), (v_hbm, v_ref), (res_hbm, res_ref), (gain_hbm, gain_ref)]
    pairs += [(group_hbm, group_ref), (roll_hbm, roll_ref)]
    at = [pl.ds(c * 256, 256) for c in range(parts)]
    pairs += [(out_proj_hbm.at[part, :], proj.at[part, :]) for part in at]
    loads = start_all(pairs + [(cot_hbm, cot_ref)], sems)
    dp, image = indices()
    tiles = []
    for low in range(0, width, 128):
        first, last = low // head, (low + 127) // head
        feature = low + iota((1, 128), 1)
        inside = [(feature >= h * head) & (feature < (h + 1) * head) for h in range(first, last + 1)]
        tiles.append((slice(low, low + 128), first, last + 1, inside))
    loads[0].wait()
    loads[1].wait()
    scores = [0.0] * HEADS
    for lanes, first, last, inside in tiles:
        q = q_ref[:, lanes]
        q = jnp.concatenate([q * one_hot(m) for m in inside], axis=0)
        part = lax.dot_general(q, k_ref[:, lanes], (((1,), (1,)), ((), ())), preferred_element_type=F32)
        for i in range(last - first):
            scores[first + i] = scores[first + i] + part[i * rows : (i + 1) * rows]
    scores = jnp.concatenate(scores, axis=0) * head ** (-0.5)
    loads[2].wait()
    counts = grid_ref[0:1, :] * grid_ref[1:2, :]
    valid = MERGE * jnp.sum(jnp.where(iota(counts.shape, 1) == image, counts, 0), axis=1, keepdims=True)
    scores = jnp.where(iota(scores.shape, 1) < valid, scores, -1e30)
    scores = jnp.exp(scores - jnp.max(scores, axis=1, keepdims=True))
    weights = (scores / jnp.sum(scores, axis=1, keepdims=True)).astype(BF16)
    loads[3].wait()
    attended = []
    for lanes, first, last, inside in tiles:
        spread = mm(weights[first * rows : last * rows], v_ref[:, lanes])
        tile = spread[:rows]
        for i in range(1, last - first):
            tile = jnp.where(inside[i], spread[i * rows : (i + 1) * rows], tile)
        attended.append(tile.astype(BF16))
    loads[6].wait()
    loads[7].wait()
    pick = pick_cotangents(dp, members, counts, roll_ref, group_ref, place_ref, cot_ref.shape[0])
    loads[4].wait()
    mixed = res_ref[...].astype(F32)
    for c in range(parts):
        loads[8 + c].wait()
        mixed = mixed + mm(jnp.concatenate(attended[2 * c : 2 * c + 2], axis=1), proj[c * 256 : (c + 1) * 256, :])
    scale = lax.rsqrt(jnp.mean(mixed * mixed, axis=1, keepdims=True) + EPSILON)
    row_valid = jnp.where(iota((rows, 1), 0) < valid, 1.0, 0.0)
    loads[5].wait()
    out_ref[...] = (mixed * scale * gain_ref[...][None, :] * row_valid).astype(BF16)
    loads[-1].wait()
    sums_ref[...] = mm(pick, cot_ref[...]).astype(BF16)


def start_all(pairs, sems):
    loads = [pltpu.make_async_copy(source, to, sems.at[i]) for i, (source, to) in enumerate(pairs)]
    for load in loads:
        load.start()
    return loads


def pick_cotangents(me, members, counts, roll_ref, group_ref, place_ref, wide):
    rollouts = roll_ref.shape[0]
    slots = wide // rollouts
    bits = shift_of(slots)
    rows = members * slots
    spread = one_hot((iota((rollouts, wide), 1) >> bits) == iota((rollouts, wide), 0))
    group = group_ref[...][None, :]
    images = group.shape[1]
    square = (images, images)
    column = jnp.sum(jnp.where(iota(square, 0) == iota(square, 1), group, 0), axis=1, keepdims=True)
    earlier = (column == group) & (iota(square, 0) < iota(square, 1))
    place = group * members + jnp.sum(jnp.where(earlier, 1, 0), axis=0, keepdims=True)
    place_ref[...] = place
    own_row = iota((rows, 1), 0)
    ours = place == me * members + (own_row >> bits)
    image = jnp.sum(jnp.where(ours, iota((rows, images), 1), 0), axis=1, keepdims=True)
    roll = roll_ref[...][None, :]
    high, low = (roll >> 8).astype(F32), (roll & 255).astype(F32)
    pair = jnp.concatenate([high, low] + [jnp.zeros((6, rollouts), F32)], axis=0).astype(BF16)
    pair = mm(pair, spread)
    roll_wide = (pair[0:1] * 256.0 + pair[1:2]).astype(I32)
    count = jnp.sum(jnp.where(ours, counts, 0), axis=1, keepdims=True)
    slot = own_row & (slots - 1)
    pick = (roll_wide == image) & (slot == (iota((1, wide), 1) & (slots - 1))) & (slot < count)
    return one_hot(pick)


def prefetch_kernel(after_ref, weight_hbm, gain_hbm, weight_ref, gain_ref, sems):
    del after_ref
    part = weight_hbm.at[pl.ds(0, weight_ref.shape[0]), :]
    for load in start_all([(part, weight_ref), (gain_hbm, gain_ref)], sems):
        load.wait()


def collect_sums(me, blocks, everything):
    rows = blocks[0].shape[0]
    for k, block in enumerate(blocks):
        everything[pl.ds(pl.multiple_of((me ^ k) * rows, rows), rows), :] = block[...]


def pick_sums(place, image, tokens, everything):
    rows, images = image.shape[0], place.shape[1]
    bits = shift_of(tokens)
    own = jnp.sum(jnp.where(iota((rows, images), 1) == image, place, 0), axis=1, keepdims=True)
    column = iota((1, everything.shape[0]), 1)
    pick = (own == (column >> bits)) & ((iota((rows, 1), 0) & (tokens - 1)) == (column & (tokens - 1)))
    return mm(one_hot(pick), everything[...])


def projection_kernel(indices, dp_count, members, sources, *refs):
    count = len(sources)
    pieces = refs[:count]
    blocks = refs[count : count + dp_count]
    weight_hbm, *weights, gain_ref, place_ref = refs[count + dp_count : count + dp_count + 4]
    outs = refs[count + dp_count + 4 :]
    messages, partial_ref, summed_ref = outs[:dp_count], outs[dp_count], outs[dp_count + 1]
    gathered, merged, sums, late_weight, sems = outs[dp_count + 2 :]
    late, chunk = late_weight.shape[0], late_weight.shape[0] // sems.shape[0]
    first = weight_hbm.shape[0] - late
    loads = start_all(
        [
            (weight_hbm.at[pl.ds(first + at, chunk), :], late_weight.at[pl.ds(at, chunk), :])
            for at in range(0, late, chunk)
        ],
        sems,
    )
    dp, mp, rep = indices()
    patches = pieces[0].shape[0] // len(sources[0])
    rep_count = members // lax.axis_size("mp")
    tokens = patches // MERGE
    width = pieces[0].shape[1]
    for piece, found in zip(pieces, sources):
        for i, (b, a) in enumerate(found):
            place = (mp ^ b) * rep_count + (rep ^ a)
            gathered[pl.ds(pl.multiple_of(place * patches, patches), patches), :] = piece[
                i * patches : (i + 1) * patches, :
            ]
    rows = members * tokens
    everything = members * patches
    to, source = iota((everything, everything), 0), iota((everything, everything), 1)
    within = to & (rows - 1)
    wanted = (
        ((within >> shift_of(tokens)) << shift_of(patches))
        + ((within & (tokens - 1)) << shift_of(MERGE))
        + (to >> shift_of(rows))
    )
    merged[...] = mm(one_hot(wanted == source), gathered[...]).astype(BF16)
    columns = weight_hbm.shape[1]
    total = jnp.zeros((rows, columns), F32)
    parts, start = [(weight, 0, weight.shape[0], None) for weight in weights], 0
    parts += [(late_weight, i * chunk, (i + 1) * chunk, load) for i, load in enumerate(loads)]
    for weight, begin, end, load in parts:
        if load is not None:
            load.wait()
        end += start - begin
        for j in range(MERGE):
            low, high = max(start, j * width), min(end, (j + 1) * width)
            if low < high:
                left = merged[j * rows : (j + 1) * rows, low - j * width : high - j * width]
                total = total + mm(left, weight[low - start + begin : high - start + begin, :])
        start = end
    hidden = total.astype(BF16)
    collect_sums(dp, blocks, sums)
    step = min(dp_count, max(1, 256 // rows))
    row = iota((step * rows, 1), 0)
    for k in range(0, dp_count, step):
        image = ((dp ^ (k + (row >> shift_of(rows)))) << shift_of(members)) + (
            (row >> shift_of(tokens)) & (members - 1)
        )
        picked = pick_sums(place_ref[...], image, tokens, sums) * gain_ref[...][None, :]
        summed_ref[k * rows : (k + step) * rows, :] = picked
    summed = summed_ref[0:rows, :]
    wide = hidden.astype(F32)
    squares = jnp.sum(wide * wide, axis=1, keepdims=True)
    inner = jnp.sum(summed * wide, axis=1, keepdims=True)
    diagonal = iota((rows, rows), 0) == iota((rows, rows), 1)
    both = jnp.concatenate(
        [jnp.sum(jnp.where(diagonal, x, 0.0), axis=0, keepdims=True) for x in (squares, inner)], axis=0
    )
    partial_ref[...] = jnp.broadcast_to(both[None], partial_ref.shape)
    share = MERGE * width // dp_count
    per_patch = width // share
    for k, message in enumerate(messages):
        message[:, 0:columns] = hidden
        target = dp ^ k
        first = pl.multiple_of((target >> shift_of(per_patch)) * rows, rows)
        for q in range(per_patch):

            @pl.when((target & (per_patch - 1)) == q)
            def _():
                message[:, columns : columns + share] = merged[
                    pl.ds(first, rows), q * share : (q + 1) * share
                ]


def final_kernel(dp_index, dp_count, model_width, *refs):
    messages = refs[:dp_count]
    summed_ref, partial_ref, gain_ref, place_ref = refs[dp_count : dp_count + 4]
    normed_ref, grad_hbm, token_grad, grad, sems = refs[dp_count + 4 :]
    me = dp_index()
    rows, columns = normed_ref.shape
    members = partial_ref.shape[0] // dp_count
    share = grad.shape[0]
    tokens = rows // members
    gain = gain_ref[...][None, :]
    place = place_ref[...]
    images = place.shape[1]
    diagonal = iota((rows, rows), 0) == iota((rows, rows), 1)
    inverses, factors = [], []
    for k in range(dp_count):
        both = jnp.sum(partial_ref[pl.ds(pl.multiple_of((me ^ k) * members, members), members)], axis=0)
        inverse = lax.rsqrt(both[0:1] / model_width + EPSILON)
        inverses.append(inverse)
        factors.append(inverse * inverse * inverse / model_width * both[1:2])
    upright = lambda x: jnp.sum(jnp.where(diagonal, x, 0.0), axis=1, keepdims=True)
    step = min(dp_count, max(1, 256 // rows))
    for k in range(0, dp_count, step):
        span = step * rows
        inverse, factor, hidden = (
            jnp.concatenate(x, axis=0)
            for x in (
                [upright(x) for x in inverses[k : k + step]],
                [upright(x) for x in factors[k : k + step]],
                [m[:, 0:columns] for m in messages[k : k + step]],
            )
        )
        token_grad[k * rows : k * rows + span, :] = (
            inverse * summed_ref[k * rows : k * rows + span, :] - hidden.astype(F32) * factor
        ).astype(BF16)
    copies = []
    chunk = min(share, 128)
    for c, at in enumerate(range(0, share, chunk)):
        size = min(chunk, share - at)
        left = jnp.concatenate([m[:, columns + at : columns + at + size] for m in messages], axis=0)
        grad[at : at + size, :] = lax.dot_general(
            left, token_grad[...], (((0,), (0,)), ((), ())), preferred_element_type=F32
        )
        copies.append(pltpu.make_async_copy(grad.at[pl.ds(at, size), :], grad_hbm.at[pl.ds(at, size), :], sems.at[c]))
        copies[-1].start()
    slot = jnp.broadcast_to(place - me * members, (8, images))
    slot = jnp.where((slot >= 0) & (slot < members), slot, -1).astype(F32).astype(BF16)
    column = iota((images, dp_count * rows), 1)
    image = ((me ^ (column >> shift_of(rows))) << shift_of(members)) + (
        (column >> shift_of(tokens)) & (members - 1)
    )
    slot = mm(slot, one_hot(image == iota((images, dp_count * rows), 0)))[0:1]
    row, column = iota((rows, dp_count * rows), 0), iota((rows, dp_count * rows), 1)
    pick = (slot == (row >> shift_of(tokens)).astype(F32)) & ((row & (tokens - 1)) == (column & (tokens - 1)))
    inverse = jnp.sum(jnp.where(pick, jnp.concatenate(inverses, axis=1), 0.0), axis=1, keepdims=True)
    pick = one_hot(pick)
    hidden = jnp.zeros((rows, columns), F32)
    for k, message in enumerate(messages):
        hidden = hidden + mm(pick[:, k * rows : (k + 1) * rows], message[:, 0:columns])
    normed_ref[...] = (hidden * inverse * gain).astype(BF16)
    for copy in copies:
        copy.wait()


def swaps(size, k):
    return [(i, i ^ k) for i in range(size)]


def on_device(
    query_rows,
    key_rows,
    value_rows,
    residual,
    out_proj,
    merge_gain,
    merger_proj,
    model_gain,
    image_grid,
    image_group,
    rollout_image,
    cotangent,
):
    dp_count, mp_count, rep_count = (lax.axis_size(a) for a in ("dp", "mp", "rep"))
    members = mp_count * rep_count
    patches, width = query_rows.shape
    tokens = patches // MERGE
    rows = members * tokens
    columns = merger_proj.shape[1]
    share = MERGE * width // dp_count
    devices = dp_count * members
    vmem, hbm = (pl.BlockSpec(memory_space=m) for m in (pltpu.VMEM, pltpu.HBM))
    scratch, dma = pltpu.VMEM, pltpu.SemaphoreType.DMA
    params = pltpu.CompilerParams(vmem_limit_bytes=VMEM_BYTES)
    stay = lambda *arrays: [pltpu.with_memory_space_constraint(x, pltpu.HBM) for x in arrays]
    grid = image_grid.T
    own = lambda: (lax.axis_index("dp"), lax.axis_index(("dp", "mp", "rep")))
    dp_index = lambda: lax.axis_index("dp")
    indices = lambda: (lax.axis_index("dp"), lax.axis_index("mp"), lax.axis_index("rep"))
    shape = jax.ShapeDtypeStruct

    images = image_group.shape[0]
    merged, sums, place = pl.pallas_call(
        functools.partial(attention_kernel, own, members),
        out_shape=[shape((patches, width), BF16), shape((rows, columns), BF16), shape((1, images), I32)],
        in_specs=[hbm] * 10,
        out_specs=[vmem] * 3,
        scratch_shapes=[scratch(grid.shape, I32)]
        + [scratch((patches, width), BF16)] * 4
        + [
            scratch((width, width), BF16),
            scratch((width,), F32),
            scratch(rollout_image.shape, I32),
            scratch((images,), I32),
            scratch(cotangent.shape, BF16),
            dma((9 + width // 256,)),
        ],
        compiler_params=params,
        name="attention",
    )(
        *stay(
            grid, query_rows, key_rows, value_rows, residual, out_proj, merge_gain, rollout_image, image_group, cotangent
        )
    )
    parts = [MERGE * width * part // sum(PARTS) for part in PARTS]

    near = 2
    far = [lax.ppermute(merged, "mp", swaps(mp_count, b)) for b in range(near, mp_count)]
    pair = jnp.concatenate(
        [merged] + [lax.ppermute(merged, "rep", swaps(rep_count, a)) for a in range(1, rep_count)], axis=0
    )
    far = jnp.concatenate(far, axis=0)
    pieces = [far] + [lax.ppermute(far, "rep", swaps(rep_count, a)) for a in range(1, rep_count)]
    pieces += [pair] + [lax.ppermute(pair, "mp", swaps(mp_count, b)) for b in range(1, near)]
    sources = [[(b, a) for b in range(near, mp_count)] for a in range(rep_count)]
    sources += [[(b, a) for a in range(rep_count)] for b in range(near)]
    blocks = {0: sums}
    for k in range(2, dp_count, 2):
        blocks[k] = lax.ppermute(sums, "dp", swaps(dp_count, k))
    for k in range(0, dp_count, 2):
        blocks[k + 1] = lax.ppermute(blocks[k], "dp", swaps(dp_count, 1))
    blocks = [blocks[k] for k in range(dp_count)]

    weight, gain = pl.pallas_call(
        prefetch_kernel,
        out_shape=[pltpu.VMEM((parts[0], columns), BF16), pltpu.VMEM(model_gain.shape, F32)],
        in_specs=[pl.BlockSpec(memory_space=pl.ANY)] + [hbm] * 2,
        out_specs=[vmem] * 2,
        scratch_shapes=[dma((2,))],
        compiler_params=params,
        cost_estimate=pl.CostEstimate(flops=0, bytes_accessed=2 * merger_proj.size, transcendentals=0),
        name="prefetch",
    )(pair, *stay(merger_proj, model_gain))

    *messages, partial, summed = pl.pallas_call(
        functools.partial(projection_kernel, indices, dp_count, members, sources),
        out_shape=[shape((rows, columns + share), BF16)] * dp_count + [shape((devices, 2, rows), F32), shape((dp_count * rows, columns), F32)],
        in_specs=[vmem] * (len(pieces) + dp_count) + [hbm] + [vmem] * 3,
        out_specs=[vmem] * (dp_count + 2),
        scratch_shapes=[
            scratch((members * patches, width), BF16),
            scratch((members * patches, width), BF16),
            scratch((dp_count * rows, columns), BF16),
            scratch((parts[1], columns), BF16),
            dma((max(1, PARTS[1] // 3),)),
        ],
        compiler_params=params,
        name="projection",
    )(*pieces, *blocks, *stay(merger_proj), weight, gain, place)

    messages = [messages[0]] + [
        lax.ppermute(messages[k], "dp", swaps(dp_count, k)) for k in range(1, dp_count)
    ]
    partial = lax.all_to_all(partial, ("dp", "mp", "rep"), split_axis=0, concat_axis=0, tiled=True)

    normed_tokens, merger_grad = pl.pallas_call(
        functools.partial(final_kernel, dp_index, dp_count, float(columns * members)),
        out_shape=[shape((rows, columns), BF16), shape((share, columns), F32)],
        in_specs=[vmem] * (dp_count + 4),
        out_specs=[vmem, hbm],
        scratch_shapes=[
            scratch((dp_count * rows, columns), BF16),
            scratch((share, columns), F32),
            dma((-(-share // 128),)),
        ],
        compiler_params=params,
        name="final",
    )(*messages, summed, partial, gain, place)
    return normed_tokens, merger_grad


def solution(mesh):
    return jax.shard_map(
        on_device,
        mesh=mesh,
        in_specs=(
            P(("dp", "mp", "rep"), None),
            P(("dp", "mp", "rep"), None),
            P(("dp", "mp", "rep"), None),
            P(("dp", "mp", "rep"), None),
            P(),
            P(),
            P(None, ("mp", "rep")),
            P(("mp", "rep")),
            P(),
            P(),
            P("dp"),
            P("dp", ("mp", "rep")),
        ),
        out_specs=(P("dp", ("mp", "rep")), P("dp", ("mp", "rep"))),
        check_vma=False,
    )
```
